256 devices in a mesh: scene: 64 (over x, z, core), strip: 4 (over y).
Axes of the slice: x: 4, y: 4, z: 8, core: 2. Of those that a mesh axis runs over, the one named last changes fastest.
Arguments:
- scene_tiles: bfloat16 [384, 10, 2, 4096], P('scene', None, None, 'strip')
- scene_slot: int32 [320], replicated, may hold values from 0 to 383, as said below
- pair_ref: int32 [4096], P('scene'), may hold values from 0 to 319, as said below
- pair_sec: int32 [4096], P('scene'), may hold values from 0 to 319, as said below
- pair_count: int32 [64], P('scene'), may hold values from 1 to 64, 2560 in all
Outputs:
- coherence: float32 [4096, 2, 2, 1024], P('scene', None, None, 'strip')
The draws below stay inside these ranges and needn't reach their ends.
Inputs may be any that keep to these rules, and one draw needn't show every extreme that they name: `scene_slot`: distinct slots; each block of 6 aligned slots holds at least one scene. `pair_ref`: within the 64 pair slots of one index of scene, the reference and secondary scenes held in the slots of any one index of scene are used at most 2 times together, and exactly so for some; a pair's two scenes differ. `pair_sec`: see pair_ref.
All inputs are finite; a program needn't handle non-finite values. No bound on the sum of `pair_count` on one device may be relied on, other than what follows from the above.
Results may differ from the reference program's by a relative error of at most 0.0003.
Values may be sent and summed in bfloat16 or wider, within the bound.
A program may use at most 64 MiB of HBM per device.

```python
import math
import jax
import jax.numpy as jnp
import numpy as np
from jax import lax

RG = 4096
AZ = 10
SLOT_DEV = 6
PCAP = 64
OWNERS = 64
SLOTS = 384
SCENES = 320
PAIR_SLOTS = 4096
PAIRS = 2560


def slots_of(key):
    key = jax.random.fold_in(key, 11)
    rest_key = jax.random.fold_in(key, 1)
    order_key = jax.random.fold_in(key, 2)
    firsts = jnp.arange(OWNERS, dtype=jnp.int32) * SLOT_DEV
    others = jnp.arange(OWNERS * (SLOT_DEV - 1), dtype=jnp.int32)
    others = others // (SLOT_DEV - 1) * SLOT_DEV + others % (SLOT_DEV - 1) + 1
    others = jax.random.permutation(rest_key, others)[:SCENES - OWNERS]
    every = jnp.concatenate([firsts, others])
    return jax.random.permutation(order_key, every).astype(jnp.int32)


def pairs_of(key):
    slots = slots_of(key)
    owner = slots // SLOT_DEV
    key = jax.random.fold_in(key, 12)
    perm_key, score_key = jax.random.split(key)
    orders = jax.vmap(lambda part_key: jax.random.permutation(part_key, OWNERS))(jax.random.split(perm_key, OWNERS))
    listed = orders[:, jnp.arange(2 * PCAP) % OWNERS]
    wanted = jnp.transpose(listed.reshape(OWNERS, PCAP, 2), (0, 2, 1))
    scores = jax.random.randint(score_key, (OWNERS, 2, PCAP, SCENES), 0, 1 << 20) * SCENES + jnp.arange(SCENES, dtype=jnp.int32)
    masked = jnp.where(owner[None, None, None, :] == wanted[..., None], scores, -1)
    picks = jnp.argmax(masked, axis=-1).astype(jnp.int32)
    return (picks[:, 0, :].reshape(-1), picks[:, 1, :].reshape(-1))


def draw_scene_slot(key, part):
    return slots_of(key)


def draw_pair_ref(key, part):
    return pairs_of(key)[0]


def draw_pair_sec(key, part):
    return pairs_of(key)[1]


def draw_scene_tiles(key, part):
    key = jax.random.fold_in(key, 13)
    common_key, noise_key, amp_key, angle_key = jax.random.split(key, 4)
    common = jax.random.normal(common_key, (AZ, 2, RG))
    noise = jax.random.normal(noise_key, (SLOTS, AZ, 2, RG))
    amp = jnp.exp(jax.random.uniform(amp_key, (SLOTS, 1, 1, 1), minval=-0.7, maxval=0.7))
    rows = jnp.ones((1, AZ, 1, 1), jnp.float32)
    angle = jax.random.uniform(angle_key, (SLOTS, 1, 1), minval=-3.14159, maxval=3.14159)
    turned_re = jnp.cos(angle) * common[None, :, 0, :] - jnp.sin(angle) * common[None, :, 1, :]
    turned_im = jnp.sin(angle) * common[None, :, 0, :] + jnp.cos(angle) * common[None, :, 1, :]
    turned = jnp.stack([turned_re, turned_im], axis=2)
    field = amp * rows * (0.8 * turned + 0.6 * noise)
    return field.astype(jnp.bfloat16)


def length_profile(amount, total, reach, slope):
    portions = [(1 << 20) // math.isqrt(rank ** slope) + 1 for rank in range(2, amount + 1)]
    surplus, given = total - reach - (amount - 1), [1] * (amount - 1)
    while surplus > 0:
        candidates = [i for i in range(amount - 1) if given[i] < reach]
        whole, remaining = sum([portions[i] for i in candidates]), surplus
        for i in candidates:
            extra = min(reach - given[i], max(1, remaining * portions[i] // whole), surplus)
            given[i] = given[i] + extra
            surplus = surplus - extra
    return np.array([reach] + given)


def ragged_sizes(rng, amount, total, reach, skew):
    if amount == 2:
        one = jax.random.randint(rng, (), max(1, total - reach), min(reach, total - 1) + 1)
        return jnp.stack([one, total - one])
    tallies = jnp.asarray(length_profile(amount, total, reach, skew), jnp.int32)
    pairs = (amount - 1) // 2
    donor, taker = tallies[1:1 + 2 * pairs:2], tallies[2:2 + 2 * pairs:2]
    slack = jnp.minimum(donor - 1, reach - taker)
    passed = jax.random.randint(jax.random.fold_in(rng, 1), (pairs,), 0, 1 << 20) % (slack + 1)
    tallies = tallies.at[1:1 + 2 * pairs:2].set(donor - passed).at[2:2 + 2 * pairs:2].set(taker + passed)
    return tallies[jax.random.permutation(jax.random.fold_in(rng, 2), amount)]


def setup_inputs(seed: int = 0) -> dict:
    splits = jax.random.split(jax.random.key(seed), 6)
    scene_tiles = draw_scene_tiles(jax.random.fold_in(splits[5], 71), 0)
    scene_slot = draw_scene_slot(jax.random.fold_in(splits[5], 71), 0)
    pair_ref = draw_pair_ref(jax.random.fold_in(splits[5], 71), 0)
    pair_sec = draw_pair_sec(jax.random.fold_in(splits[5], 71), 0)
    pair_count = ragged_sizes(splits[4], OWNERS, PAIRS, PCAP, 2).astype(jnp.int32)
    return dict(scene_tiles=scene_tiles, scene_slot=scene_slot, pair_ref=pair_ref, pair_sec=pair_sec, pair_count=pair_count)


def one_pair(tile_a, tile_b):
    a0 = tile_a[:, 0].astype(jnp.float32)
    a1 = tile_a[:, 1].astype(jnp.float32)
    b0 = tile_b[:, 0].astype(jnp.float32)
    b1 = tile_b[:, 1].astype(jnp.float32)
    planes = jnp.stack([a0 * b0 + a1 * b1, a1 * b0 - a0 * b1, a0 * a0 + a1 * a1, b0 * b0 + b1 * b1])
    lines = planes.reshape(4, AZ // 5, 5, RG).sum(axis=2)
    padded = jnp.pad(lines, ((0, 0), (0, 0), (10, 10)))
    blocks = padded.reshape(4, AZ // 5, (RG + 20) // 4, 4).sum(axis=3)
    count = RG // 4
    looks = blocks[:, :, 0:count] + blocks[:, :, 1:count + 1] + blocks[:, :, 2:count + 2] + blocks[:, :, 3:count + 3] + blocks[:, :, 4:count + 4]
    denom = jnp.sqrt(looks[2] * looks[3] + 1e-06)
    return jnp.stack([looks[0] / denom, looks[1] / denom], axis=1)

def reference(scene_tiles, scene_slot, pair_ref, pair_sec, pair_count):

    def run(index):
        tile_a = scene_tiles[scene_slot[pair_ref[index]]]
        tile_b = scene_tiles[scene_slot[pair_sec[index]]]
        result = one_pair(tile_a, tile_b)
        live = index % PCAP < pair_count[index // PCAP]
        return jnp.where(live, result, jnp.zeros_like(result))
    return lax.map(run, jnp.arange(PAIR_SLOTS, dtype=jnp.int32))
```

```python
import functools

import jax
import jax.numpy as jnp
import numpy as np
from jax import lax
from jax.experimental import pallas as pl
from jax.experimental.pallas import tpu as pltpu
from jax.sharding import PartitionSpec as P

MESH = pl.DeviceIdType.MESH
F32 = jnp.float32
BF16 = jnp.bfloat16

XS, ZS, CHIPS = 4, 8, 32
STRIPS = 4
SLOTS = 6
AZ = 5
TILES = 8
ROWS = 480


def feature_order():
    order = np.zeros((ROWS, 512), np.float32)
    for az in range(AZ):
        for ri in range(2):
            for cell in range(-10, 38):
                block, w = (cell + 2) // 4, (cell + 2) % 4
                base = 96 * az + 48 * ri
                if 0 <= block < 8:
                    row = base + 8 * w + block
                else:
                    row = base + 32 + 4 * w + {-2: 0, -1: 1, 8: 2, 9: 3}[block]
                if 0 <= cell < 32:
                    lane = 32 * (2 * az + ri) + cell
                else:
                    h = cell + 10 if cell < 0 else cell - 22
                    lane = 32 * (10 + az) + 16 * ri + h
                order[row, lane] = 1.0
    return order


def far_first(i):
    return jnp.where(i == 0, 2, jnp.where(i == 1, 1, jnp.where(i == 2, 3, 0)))


def windows(main, halo):
    row = lax.broadcasted_iota(jnp.int32, main.shape, 0)
    total = main + jnp.where(row < 1, pltpu.roll(halo, 7, 0), pltpu.roll(main, 1, 0))
    total += jnp.where(row < 2, halo, pltpu.roll(main, 2, 0))
    total += jnp.where(row >= 7, pltpu.roll(halo, 1, 0), pltpu.roll(main, 7, 0))
    total += jnp.where(row >= 6, halo, pltpu.roll(main, 6, 0))
    return total


def kernel(
    tiles_ref, slot_ref, list_ref, order_ref, out_ref,
    ext, msg, land, lst, chip_list, lists, scene_k, hot, feat, both, res, back, turned, fin,
    own_sem, core_send, core_recv, edge_send, edge_recv, list_send, list_recv,
    data_send, data_recv, back_send, back_recv,
):
    me = lax.axis_index("scene")
    y = lax.axis_index("strip")
    chip, c = me // 2, lax.rem(me, 2)
    other = 1 - c
    x, z = chip // ZS, lax.rem(chip, ZS)
    up, down = lax.rem(y + 1, STRIPS), lax.rem(y + STRIPS - 1, STRIPS)
    partner = {"scene": chip * 2 + other}

    barrier = pltpu.get_barrier_semaphore()

    def greet(k, carry):
        @pl.when(k != chip)
        def _():
            pl.semaphore_signal(barrier, inc=1, device_id={"scene": 2 * k + c}, device_id_type=MESH)
        return carry

    lax.fori_loop(0, CHIPS, greet, 0)
    pl.semaphore_signal(barrier, inc=1, device_id=partner, device_id_type=MESH)
    for row in (up, down):
        for core in (c, other):
            pl.semaphore_signal(
                barrier, inc=1, device_id={"scene": chip * 2 + core, "strip": row}, device_id_type=MESH
            )

    own = pltpu.make_async_copy(tiles_ref.at[c], ext.at[c, :, :, pl.ds(128, 1024)], own_sem)
    own.start()

    rows = lax.broadcasted_iota(jnp.int32, (512, 384), 0)
    place = lax.rem(rows, 8)
    slot = (rows // 16) * 12 + (lax.rem(rows, 16) // 8) * 6 + place
    slot = jnp.where(place < SLOTS, slot, -7)
    lane = lax.broadcasted_iota(jnp.int32, (512, 384), 1).astype(F32)
    scene = jnp.sum(jnp.where(slot == slot_ref[...], lane + 1.0, 0.0), axis=1, keepdims=True) - 1.0
    scene_k[...] = jnp.broadcast_to(scene, (512, 128)).astype(jnp.int32)

    pl.semaphore_wait(barrier, CHIPS - 1 + 1 + 4)

    give_list = pltpu.make_async_remote_copy(
        src_ref=list_ref, dst_ref=lst, send_sem=core_send.at[0], recv_sem=core_recv.at[0],
        device_id=partner, device_id_type=MESH,
    )
    give_list.start()
    give_line = pltpu.make_async_remote_copy(
        src_ref=tiles_ref.at[other], dst_ref=ext.at[c, :, :, pl.ds(128, 1024)],
        send_sem=core_send.at[1], recv_sem=core_recv.at[1], device_id=partner, device_id_type=MESH,
    )
    give_line.start()
    edges = []
    for side, (row, src, dst) in enumerate(((up, 896, 0), (down, 0, 1152))):
        for n, core in enumerate((c, other)):
            copy = pltpu.make_async_remote_copy(
                src_ref=tiles_ref.at[core, :, :, pl.ds(src, 128)],
                dst_ref=ext.at[c, :, :, pl.ds(dst, 128)],
                send_sem=edge_send.at[2 * side + n],
                recv_sem=edge_recv.at[2 * side + n],
                device_id={"scene": chip * 2 + core, "strip": row},
                device_id_type=MESH,
            )
            copy.start()
            edges.append(copy)

    give_list.wait()
    half = lax.broadcasted_iota(jnp.int32, (2, 128), 1) // 64
    chip_list[...] = jnp.where(half == c, list_ref[...], lst[...])
    lists[chip] = chip_list[...]

    def list_copy(k):
        return pltpu.make_async_remote_copy(
            src_ref=chip_list, dst_ref=lists.at[chip], send_sem=list_send.at[k], recv_sem=list_recv.at[chip],
            device_id={"scene": 2 * k + c}, device_id_type=MESH,
        )

    def send_list(i, carry):
        k = lax.rem(x + far_first(i // ZS), XS) * ZS + lax.rem(z + 4 + i, ZS)

        @pl.when(k != chip)
        def _():
            list_copy(k).start()
        return carry

    lax.fori_loop(0, CHIPS, send_list, 0)

    own.wait()
    give_line.wait()
    for copy in edges:
        copy.wait()

    @pl.when(y == 0)
    def _():
        ext[:, :, :, 0:128] = jnp.zeros((2, AZ, 16, 128), BF16)

    @pl.when(y == STRIPS - 1)
    def _():
        ext[:, :, :, 1152:1280] = jnp.zeros((2, AZ, 16, 128), BF16)

    lanes = lax.broadcasted_iota(jnp.int32, (16, 128), 1)
    in32 = lax.rem(lanes, 32)
    row8 = lax.broadcasted_iota(jnp.int32, (2, 8, 128), 1)

    def data_copy(k):
        return pltpu.make_async_remote_copy(
            src_ref=msg.at[k], dst_ref=land.at[chip], send_sem=data_send.at[k], recv_sem=data_recv.at[chip],
            device_id={"scene": 2 * k + c}, device_id_type=MESH,
        )

    def pack(i, carry):
        first = 1 - z // 4
        h = jnp.where(lax.rem(i, 2) == 0, first, 1 - first)
        t = lax.rem(x + far_first(i // 2), XS) * 2 + h
        at = pl.ds(pl.multiple_of(t * 128, 128), 384)
        groups, halos = [], []
        for az in range(AZ):
            v = [ext[core, az, :, at].astype(F32) for core in range(2)]
            re = jnp.concatenate([v[0][0:8], v[1][0:8]], axis=0)
            im = jnp.concatenate([v[0][8:16], v[1][8:16]], axis=0)
            groups += [re[:, 128:256], im[:, 128:256]]
            near = jnp.where(in32 < 10, pltpu.roll(re, 10, 1)[:, 128:256], pltpu.roll(re, 384 - 22, 1)[:, 128:256])
            far = jnp.where(in32 < 26, pltpu.roll(im, 26, 1)[:, 128:256], pltpu.roll(im, 384 - 6, 1)[:, 128:256])
            halos.append(jnp.where(in32 < 16, near, far))
        groups += halos + [jnp.zeros((16, 128), F32)]
        turned4 = []
        for s in range(4):
            g = groups[4 * s : 4 * s + 4]
            low = lanes < 64
            for a, b in ((0, 2), (1, 3)):
                ga, gb = g[a], g[b]
                g[a] = jnp.where(low, ga, pltpu.roll(gb, 64, 1))
                g[b] = jnp.where(low, pltpu.roll(ga, 64, 1), gb)
            low = lax.rem(lanes, 64) < 32
            for a, b in ((0, 1), (2, 3)):
                ga, gb = g[a], g[b]
                g[a] = jnp.where(low, ga, pltpu.roll(gb, 32, 1))
                g[b] = jnp.where(low, pltpu.roll(ga, 96, 1), gb)
            turned4.append(g)
        for sub in range(4):
            k = 4 * t + sub
            last = turned4[3][sub].reshape(2, 8, 128)
            for s in range(3):
                tile = turned4[s][sub].reshape(2, 8, 128)
                tile = jnp.where(row8 >= 6, pltpu.roll(last, 6 - 2 * s, 1), tile)
                msg[k, :, 128 * s : 128 * s + 128] = tile.reshape(16, 128).astype(BF16)

            @pl.when(k != chip)
            def _():
                data_copy(k).start()
        return carry

    lax.fori_loop(0, TILES, pack, 0)
    land[chip] = msg[chip]

    def get_list(k, carry):
        @pl.when(k != chip)
        def _():
            pltpu.make_async_remote_copy(
                src_ref=chip_list, dst_ref=lists.at[k], send_sem=list_send.at[k], recv_sem=list_recv.at[k],
                device_id={"scene": 2 * k + c}, device_id_type=MESH,
            ).wait()
        return carry

    lax.fori_loop(0, CHIPS, get_list, 0)

    def one_hot(m, carry):
        for n in range(2):
            pair = lists[2 * m + n]
            for part in range(2):
                hit = jnp.where(scene_k[...] == pair[part : part + 1, :], 1.0, 0.0).astype(BF16)
                hot[m, :, 256 * part + 128 * n : 256 * part + 128 * n + 128] = hit
        return carry

    lax.fori_loop(0, CHIPS // 2, one_hot, 0)

    def get_data(k, carry):
        @pl.when(k != chip)
        def _():
            pltpu.make_async_remote_copy(
                src_ref=msg.at[k], dst_ref=land.at[k], send_sem=data_send.at[k], recv_sem=data_recv.at[k],
                device_id={"scene": 2 * k + c}, device_id_type=MESH,
            ).wait()
        return carry

    lax.fori_loop(0, CHIPS, get_data, 0)

    part = [land[:, :, 128 * s : 128 * s + 128].reshape(512, 128) for s in range(3)]
    wide = [p.astype(F32).reshape(64, 8, 128) for p in part]
    row = lax.broadcasted_iota(jnp.int32, (64, 8, 128), 1)
    last = jnp.where(
        row < 2, pltpu.roll(wide[0], 2, 1), jnp.where(row < 4, pltpu.roll(wide[1], 4, 1), pltpu.roll(wide[2], 6, 1))
    )
    sent = jnp.concatenate(part + [last.reshape(512, 128).astype(BF16)], axis=1)
    feat[...] = lax.dot_general(
        order_ref[...], sent, (((1,), (1,)), ((), ())), preferred_element_type=F32
    ).astype(BF16)

    def back_copy(k):
        return pltpu.make_async_remote_copy(
            src_ref=res.at[k], dst_ref=back.at[chip], send_sem=back_send.at[k], recv_sem=back_recv.at[chip],
            device_id={"scene": 2 * k + c}, device_id_type=MESH,
        )

    def compute(i, carry):
        zp = lax.rem(z // 2 + far_first(lax.rem(i, 4)), 4)
        m = lax.rem(x + far_first(i // 4), XS) * 4 + zp
        both[...] = jnp.dot(feat[...], hot[m], preferred_element_type=F32)
        main, halo = [0.0] * 4, [0.0] * 4
        for az in range(AZ):
            a0, b0 = both[96 * az : 96 * az + 48, 0:256], both[96 * az : 96 * az + 48, 256:512]
            a1, b1 = both[96 * az + 48 : 96 * az + 96, 0:256], both[96 * az + 48 : 96 * az + 96, 256:512]
            planes = (a0 * b0 + a1 * b1, a1 * b0 - a0 * b1, a0 * a0 + a1 * a1, b0 * b0 + b1 * b1)
            for n, plane in enumerate(planes):
                for w in range(4):
                    main[n] = main[n] + plane[8 * w : 8 * w + 8]
                for w in range(4, 6):
                    halo[n] = halo[n] + plane[8 * w : 8 * w + 8]
        looks = [windows(u, v + pltpu.roll(v, 4, 0)) for u, v in zip(main, halo)]
        scale = lax.rsqrt(looks[2] * looks[3] + 1e-06)
        value = jnp.concatenate([looks[0] * scale, looks[1] * scale], axis=0)
        for n in range(2):
            k = 2 * m + n
            res[k] = value[:, 128 * n : 128 * n + 128]

            @pl.when(k != chip)
            def _():
                back_copy(k).start()
        return carry

    lax.fori_loop(0, CHIPS // 2, compute, 0)
    back[chip] = res[chip]

    def get_back(k, carry):
        @pl.when(k != chip)
        def _():
            pltpu.make_async_remote_copy(
                src_ref=res.at[k], dst_ref=back.at[k], send_sem=back_send.at[k], recv_sem=back_recv.at[k],
                device_id={"scene": 2 * k + c}, device_id_type=MESH,
            ).wait()
        return carry

    lax.fori_loop(0, CHIPS, get_back, 0)

    for ri in range(2):
        turned[ri] = back[:, 8 * ri : 8 * ri + 8, :].reshape(256, 128).T
    give = pltpu.make_async_remote_copy(
        src_ref=turned.at[:, pl.ds(pl.multiple_of(64 * other, 64), 64), :], dst_ref=fin,
        send_sem=core_send.at[2], recv_sem=core_recv.at[2], device_id=partner, device_id_type=MESH,
    )
    give.start()
    out_ref[c] = turned[:, pl.ds(pl.multiple_of(64 * c, 64), 64), :]
    give.wait()
    out_ref[other] = fin[...]


def shards(scene_tiles, scene_slot, pair_ref, pair_sec, pair_count):
    pcap = pair_ref.shape[0]
    tiles = jnp.pad(scene_tiles, ((0, 2), (0, 0), (0, 0), (0, 0)))
    tiles = tiles.reshape(8, 2, AZ, 2, 1024).transpose(1, 2, 3, 0, 4).reshape(2, AZ, 16, 1024)
    slots = jnp.pad(scene_slot, (0, 64), constant_values=-9).reshape(1, 384)
    live = jnp.arange(pcap, dtype=jnp.int32) < pair_count[0]
    pairs = jnp.where(live, jnp.stack([pair_ref, pair_sec]), -2)
    pairs = jnp.concatenate([pairs, pairs], axis=1)
    order = jnp.asarray(feature_order(), BF16)
    vmem = pl.BlockSpec(memory_space=pltpu.VMEM)
    dma = pltpu.SemaphoreType.DMA
    out = pl.pallas_call(
        kernel,
        out_shape=jax.ShapeDtypeStruct((2, 2, pcap, 256), F32),
        in_specs=[vmem] * 4,
        out_specs=vmem,
        scratch_shapes=[
            pltpu.VMEM((2, AZ, 16, 1280), BF16),
            pltpu.VMEM((CHIPS, 16, 384), BF16),
            pltpu.VMEM((CHIPS, 16, 384), BF16),
            pltpu.VMEM((2, 128), jnp.int32),
            pltpu.VMEM((2, 128), jnp.int32),
            pltpu.VMEM((CHIPS, 2, 128), jnp.int32),
            pltpu.VMEM((512, 128), jnp.int32),
            pltpu.VMEM((CHIPS // 2, 512, 512), BF16),
            pltpu.VMEM((ROWS, 512), BF16),
            pltpu.VMEM((ROWS, 512), F32),
            pltpu.VMEM((CHIPS, 16, 128), F32),
            pltpu.VMEM((CHIPS, 16, 128), F32),
            pltpu.VMEM((2, 128, 256), F32),
            pltpu.VMEM((2, 64, 256), F32),
            dma, dma((3,)), dma((3,)), dma((4,)), dma((4,)), dma((CHIPS,)), dma((CHIPS,)),
            dma((CHIPS,)), dma((CHIPS,)), dma((CHIPS,)), dma((CHIPS,)),
        ],
        compiler_params=pltpu.CompilerParams(
            collective_id=0, has_side_effects=True, vmem_limit_bytes=48 << 20
        ),
        name="coherence",
    )(tiles, slots, pairs, order)
    return out.transpose(2, 0, 1, 3)


def solution(mesh):
    placed = (P("scene", None, None, "strip"), P(), P("scene"), P("scene"), P("scene"))
    return jax.shard_map(
        shards,
        mesh=mesh,
        in_specs=placed,
        out_specs=P("scene", None, None, "strip"),
        check_vma=False,
    )
```

```python
import functools

import jax
import jax.numpy as jnp
import numpy as np
from jax import lax
from jax.experimental import pallas as pl
from jax.experimental.pallas import tpu as pltpu
from jax.sharding import PartitionSpec as P

MESH = pl.DeviceIdType.MESH
F32 = jnp.float32
BF16 = jnp.bfloat16

XS, ZS, CHIPS = 4, 8, 32
STRIPS = 4
SLOTS = 6
AZ = 5
TILES = 8
ROWS = 480


def feature_order():
    order = np.zeros((ROWS, 512), np.float32)
    for az in range(AZ):
        for ri in range(2):
            for cell in range(-10, 38):
                block, w = (cell + 2) // 4, (cell + 2) % 4
                base = 96 * az + 48 * ri
                if 0 <= block < 8:
                    row = base + 8 * w + block
                else:
                    row = base + 32 + 4 * w + {-2: 0, -1: 1, 8: 2, 9: 3}[block]
                if 0 <= cell < 32:
                    lane = 32 * (2 * az + ri) + cell
                else:
                    h = cell + 10 if cell < 0 else cell - 22
                    lane = 32 * (10 + az) + 16 * ri + h
                order[row, lane] = 1.0
    return order


def far_first(i):
    return jnp.where(i == 0, 2, jnp.where(i == 1, 1, jnp.where(i == 2, 3, 0)))


def across(x, i):
    low = lax.rem(x, 2)
    high = x // 2
    flip = jnp.where(lax.rem(i, 3) == 0, low, 1 - low)
    return jnp.where(i < 2, 1 - high, high) * 2 + flip


def both_parts(v):
    rows = jnp.zeros((2, v.shape[-1]), F32)
    v = v.astype(F32)
    return jnp.concatenate([v[:, 0, :], rows, v[:, 1, :], rows], axis=0).astype(BF16)


def windows(main, halo):
    row = lax.broadcasted_iota(jnp.int32, main.shape, 0)
    total = main + jnp.where(row < 1, pltpu.roll(halo, 7, 0), pltpu.roll(main, 1, 0))
    total += jnp.where(row < 2, halo, pltpu.roll(main, 2, 0))
    total += jnp.where(row >= 7, pltpu.roll(halo, 1, 0), pltpu.roll(main, 7, 0))
    total += jnp.where(row >= 6, halo, pltpu.roll(main, 6, 0))
    return total


def kernel(
    tiles_hbm, slot_hbm, ref_hbm, sec_hbm, count_hbm, order_hbm, out_ref,
    slot_ref, ref_ref, sec_ref, count_ref, order_ref, raw, pre, ext, edge, edge_msg, sent, msg, land, own_list, lst, chip_list, lists, scene_k, hot, feat, both_a, both_b,
    res, back, turned, fin,
    in_sem, core_send, core_recv, edge_send, edge_recv, list_send, list_recv,
    data_send, data_recv, back_send, back_recv, fin_send, fin_recv,
):
    me = lax.axis_index("scene")
    y = lax.axis_index("strip")
    chip, c = me // 2, lax.rem(me, 2)
    other = 1 - c
    x, z = chip // ZS, lax.rem(chip, ZS)
    partner = {"scene": chip * 2 + other}

    barrier = pltpu.get_barrier_semaphore()

    def greet(k, carry):
        @pl.when(k != chip)
        def _():
            pl.semaphore_signal(barrier, inc=1, device_id={"scene": 2 * k + c}, device_id_type=MESH)
        return carry

    pl.semaphore_signal(barrier, inc=1, device_id=partner, device_id_type=MESH)
    lax.fori_loop(0, CHIPS, greet, 0)

    at_left = (chip == 0) & (y > 0)
    at_right = (chip == CHIPS - 1) & (y < STRIPS - 1)
    side = jnp.where(chip == 0, y - 1, y + 1)

    def greet_side(k, carry):
        pl.semaphore_signal(
            barrier, inc=1, device_id={"scene": 2 * k + c, "strip": side}, device_id_type=MESH
        )
        return carry

    @pl.when(at_left | at_right)
    def _():
        lax.fori_loop(0, CHIPS, greet_side, 0)

    gets = [
        pltpu.make_async_copy(src, dst, in_sem.at[n])
        for n, (src, dst) in enumerate((
            (tiles_hbm, raw), (ref_hbm, ref_ref), (sec_hbm, sec_ref), (count_hbm, count_ref),
            (slot_hbm, slot_ref), (order_hbm, order_ref),
        ))
    ]
    for get in gets:
        get.start()
    for get in gets[1:4]:
        get.wait()
    mine = lax.broadcasted_iota(jnp.int32, (1, 64), 1) < count_ref[...]
    for n, ref in enumerate((ref_ref, sec_ref)):
        pair = jnp.where(mine, ref[...], -2)
        own_list[n : n + 1, 0:64] = pair
        own_list[n : n + 1, 64:128] = pair
    ext[:, :, :, 0:128] = jnp.zeros((2, AZ, 16, 128), BF16)
    ext[:, :, :, 1152:1280] = jnp.zeros((2, AZ, 16, 128), BF16)
    gets[0].wait()

    def lines(az, carry):
        pre[az] = both_parts(raw[:, 5 * other + az])
        ext[c, az, :, 128:1152] = both_parts(raw[:, 5 * c + az])
        return carry

    lax.fori_loop(0, AZ, lines, 0)
    sides = jnp.where(y < STRIPS - 1, 1, 0) + jnp.where(y > 0, 1, 0)
    pl.semaphore_wait(barrier, CHIPS + sides)

    give_line = pltpu.make_async_remote_copy(
        src_ref=pre, dst_ref=ext.at[c, :, :, pl.ds(128, 1024)],
        send_sem=core_send.at[1], recv_sem=core_recv.at[1], device_id=partner, device_id_type=MESH,
    )
    give_line.start()
    give_list = pltpu.make_async_remote_copy(
        src_ref=own_list, dst_ref=lst, send_sem=core_send.at[0], recv_sem=core_recv.at[0],
        device_id=partner, device_id_type=MESH,
    )
    give_list.start()

    give_list.wait()
    half = lax.broadcasted_iota(jnp.int32, (2, 128), 1) // 64
    chip_list[...] = jnp.where(half == c, own_list[...], lst[...])
    lists[chip] = chip_list[...]

    def list_copy(k):
        return pltpu.make_async_remote_copy(
            src_ref=chip_list, dst_ref=lists.at[chip], send_sem=list_send.at[k], recv_sem=list_recv.at[chip],
            device_id={"scene": 2 * k + c}, device_id_type=MESH,
        )

    def send_list(i, carry):
        k = across(x, i // ZS) * ZS + lax.rem(z + 4 + i, ZS)

        @pl.when(k != chip)
        def _():
            list_copy(k).start()
        return carry

    give_line.wait()

    lanes = lax.broadcasted_iota(jnp.int32, (16, 128), 1)
    in32 = lax.rem(lanes, 32)
    row8 = lax.broadcasted_iota(jnp.int32, (2, 8, 128), 1)

    def data_copy(k):
        return pltpu.make_async_remote_copy(
            src_ref=msg.at[k], dst_ref=land.at[chip], send_sem=data_send.at[k], recv_sem=data_recv.at[chip],
            device_id={"scene": 2 * k + c}, device_id_type=MESH,
        )

    def pack(t):
        at = pl.ds(pl.multiple_of(t * 128, 128), 384)
        groups, halos = [], []
        for az in range(AZ):
            v = [ext[core, az, :, at].astype(F32) for core in range(2)]
            re = jnp.concatenate([v[0][0:8], v[1][0:8]], axis=0)
            im = jnp.concatenate([v[0][8:16], v[1][8:16]], axis=0)
            groups += [re[:, 128:256], im[:, 128:256]]
            near = jnp.where(in32 < 10, pltpu.roll(re, 10, 1)[:, 128:256], pltpu.roll(re, 384 - 22, 1)[:, 128:256])
            far = jnp.where(in32 < 26, pltpu.roll(im, 26, 1)[:, 128:256], pltpu.roll(im, 384 - 6, 1)[:, 128:256])
            halos.append(jnp.where(in32 < 16, near, far))
        groups += halos + [jnp.zeros((16, 128), F32)]
        turned4 = []
        for s in range(4):
            g = groups[4 * s : 4 * s + 4]
            low = lanes < 64
            for a, b in ((0, 2), (1, 3)):
                ga, gb = g[a], g[b]
                g[a] = jnp.where(low, ga, pltpu.roll(gb, 64, 1))
                g[b] = jnp.where(low, pltpu.roll(ga, 64, 1), gb)
            low = lax.rem(lanes, 64) < 32
            for a, b in ((0, 1), (2, 3)):
                ga, gb = g[a], g[b]
                g[a] = jnp.where(low, ga, pltpu.roll(gb, 32, 1))
                g[b] = jnp.where(low, pltpu.roll(ga, 96, 1), gb)
            turned4.append(g)
        for sub in range(4):
            k = 4 * t + sub
            last = turned4[3][sub].reshape(2, 8, 128)
            for s in range(3):
                tile = turned4[s][sub].reshape(2, 8, 128)
                tile = jnp.where(row8 >= 6, pltpu.roll(last, 6 - 2 * s, 1), tile)
                msg[k, :, 128 * s : 128 * s + 128] = tile.reshape(16, 128).astype(BF16)
        for sub in range(4):
            k = 4 * t + sub

            @pl.when(k != chip)
            def _():
                data_copy(k).start()

    def tile_at(i):
        first = 1 - z // 4
        return across(x, i // 2) * 2 + jnp.where(lax.rem(i, 2) == 0, first, 1 - first)

    def pack_at(i, carry):
        pack(tile_at(i))
        return carry

    def edge_pack(n, start):
        whole = jnp.zeros((16, 128), F32)
        for az in range(AZ):
            v = [ext[core, az, :, start : start + 128].astype(F32) for core in range(2)]
            re = jnp.concatenate([v[0][0:8], v[1][0:8]], axis=0)
            im = jnp.concatenate([v[0][8:16], v[1][8:16]], axis=0)
            for s in range(3 if az == 4 else 1):
                to = 32 * s if az == 4 else 32 * ((az + 2) % 4)
                here = jnp.where(in32 < 16, pltpu.roll(re, 10 + to, 1), pltpu.roll(im, (26 + to) % 128, 1))
                if az == 4:
                    here = pltpu.roll(here.reshape(2, 8, 128), 6 - 2 * s, 1).reshape(16, 128)
                    keep = (lanes // 32 == s) & (row8.reshape(16, 128) >= 6)
                else:
                    keep = lanes // 32 == to // 32
                whole = jnp.where(keep, here, whole)
        edge_msg[n] = whole.astype(BF16)

    def edge_copy(n, to, row):
        return pltpu.make_async_remote_copy(
            src_ref=edge_msg.at[n], dst_ref=edge.at[chip], send_sem=edge_send.at[n], recv_sem=edge_recv.at[chip],
            device_id={"scene": 2 * to + c, "strip": row}, device_id_type=MESH,
        )

    pack_at(0, 0)
    edge_pack(0, 1024)
    edge_pack(1, 128)

    @pl.when(y < STRIPS - 1)
    def _():
        edge_copy(0, 0, y + 1).start()

    @pl.when(y > 0)
    def _():
        edge_copy(1, CHIPS - 1, y - 1).start()

    lax.fori_loop(1, 3, pack_at, 0)
    lax.fori_loop(0, CHIPS, send_list, 0)
    lax.fori_loop(3, TILES, pack_at, 0)

    @pl.when(y < STRIPS - 1)
    def _():
        edge_copy(0, 0, y + 1).wait_send()

    @pl.when(y > 0)
    def _():
        edge_copy(1, CHIPS - 1, y - 1).wait_send()

    land[chip] = msg[chip]

    gets[4].wait()
    gets[5].wait()

    rows = lax.broadcasted_iota(jnp.int32, (512, 320), 0)
    place = lax.rem(rows, 8)
    slot = (rows // 16) * 12 + (lax.rem(rows, 16) // 8) * 6 + place
    slot = jnp.where(place < SLOTS, slot, -7)
    lane = lax.broadcasted_iota(jnp.int32, (512, 320), 1).astype(F32)
    scene = jnp.sum(jnp.where(slot == slot_ref[...].reshape(1, 320), lane + 1.0, 0.0), axis=1, keepdims=True) - 1.0
    scene_k[...] = jnp.broadcast_to(scene, (512, 128)).astype(jnp.int32)

    def get_list(k, carry):
        @pl.when(k != chip)
        def _():
            pltpu.make_async_remote_copy(
                src_ref=chip_list, dst_ref=lists.at[k], send_sem=list_send.at[k], recv_sem=list_recv.at[k],
                device_id={"scene": 2 * k + c}, device_id_type=MESH,
            ).wait()
        return carry

    lax.fori_loop(0, CHIPS, get_list, 0)

    def one_hot(m, carry):
        for n in range(2):
            pair = lists[2 * m + n]
            for part in range(2):
                hit = jnp.where(scene_k[...] == pair[part : part + 1, :], 1.0, 0.0).astype(BF16)
                hot[m, :, 256 * part + 128 * n : 256 * part + 128 * n + 128] = hit
        return carry

    lax.fori_loop(0, CHIPS // 2, one_hot, 0)

    def get_data(k, carry):
        @pl.when(k != chip)
        def _():
            pltpu.make_async_remote_copy(
                src_ref=msg.at[k], dst_ref=land.at[k], send_sem=data_send.at[k], recv_sem=data_recv.at[k],
                device_id={"scene": 2 * k + c}, device_id_type=MESH,
            ).wait()
        return carry

    lax.fori_loop(0, CHIPS, get_data, 0)

    part = [land[:, :, 128 * s : 128 * s + 128].reshape(512, 128) for s in range(3)]
    wide = [p.astype(F32).reshape(64, 8, 128) for p in part]
    row = lax.broadcasted_iota(jnp.int32, (64, 8, 128), 1)
    last = jnp.where(
        row < 2, pltpu.roll(wide[0], 2, 1), jnp.where(row < 4, pltpu.roll(wide[1], 4, 1), pltpu.roll(wide[2], 6, 1))
    )
    sent[...] = jnp.concatenate(part + [last.reshape(512, 128).astype(BF16)], axis=1)

    def get_edge(k, carry):
        pltpu.make_async_remote_copy(
            src_ref=edge_msg.at[0], dst_ref=edge.at[k], send_sem=edge_send.at[0], recv_sem=edge_recv.at[k],
            device_id={"scene": 2 * k + c, "strip": side}, device_id_type=MESH,
        ).wait_recv()
        return carry

    @pl.when(at_left | at_right)
    def _():
        lax.fori_loop(0, CHIPS, get_edge, 0)
        lane = lax.broadcasted_iota(jnp.int32, (512, 128), 1)
        left = jnp.where(chip == 0, 1, 0)
        ours = jnp.where(lax.rem(lane, 16) < 10, left, 1 - left) == 1
        got = edge[...].astype(F32).reshape(512, 128)
        fold = got.reshape(64, 8, 128)
        deep = [pltpu.roll(fold, 2 * s + 2, 1).reshape(512, 128) for s in range(3)]
        deep = [pltpu.roll(deep[s], 64 - 32 * s, 1) for s in range(3)]
        level = row.reshape(512, 128)
        deep = jnp.where(level < 2, deep[0], jnp.where(level < 4, deep[1], deep[2]))
        third, fourth = sent[:, 256:384].astype(F32), sent[:, 384:512].astype(F32)
        sent[:, 256:384] = jnp.where(ours & (lane >= 64), got, third).astype(BF16)
        sent[:, 384:512] = jnp.where(ours, jnp.where(lane < 64, got, deep), fourth).astype(BF16)

    feat[...] = lax.dot_general(
        order_ref[...], sent[...], (((1,), (1,)), ((), ())), preferred_element_type=F32
    ).astype(BF16)

    def back_copy(k):
        return pltpu.make_async_remote_copy(
            src_ref=res.at[k], dst_ref=back.at[chip], send_sem=back_send.at[k], recv_sem=back_recv.at[chip],
            device_id={"scene": 2 * k + c}, device_id_type=MESH,
        )

    def step_of(i):
        zp = lax.rem(z // 2 + far_first(lax.rem(i, 4)), 4)
        return across(x, i // 4) * 4 + zp

    def gather(ref, i):
        ref[...] = jnp.dot(feat[...], hot[step_of(i)], preferred_element_type=F32)

    def sums(ref, i):
        main, halo = [0.0] * 4, [0.0] * 4
        for az in range(AZ):
            a0, b0 = ref[96 * az : 96 * az + 48, 0:256], ref[96 * az : 96 * az + 48, 256:512]
            a1, b1 = ref[96 * az + 48 : 96 * az + 96, 0:256], ref[96 * az + 48 : 96 * az + 96, 256:512]
            planes = (a0 * b0 + a1 * b1, a1 * b0 - a0 * b1, a0 * a0 + a1 * a1, b0 * b0 + b1 * b1)
            for n, plane in enumerate(planes):
                for w in range(4):
                    main[n] = main[n] + plane[8 * w : 8 * w + 8]
                for w in range(4, 6):
                    halo[n] = halo[n] + plane[8 * w : 8 * w + 8]
        looks = [windows(u, v + pltpu.roll(v, 4, 0)) for u, v in zip(main, halo)]
        scale = lax.rsqrt(looks[2] * looks[3] + 1e-06)
        value = jnp.concatenate([looks[0] * scale, looks[1] * scale], axis=0)
        k = 2 * step_of(i)
        res[k] = value[:, 0:128]
        res[k + 1] = value[:, 128:256]

    gather(both_a, 0)

    def compute(j, carry):
        i = 2 * j
        gather(both_b, i + 1)
        sums(both_a, i)
        gather(both_a, lax.rem(i + 2, CHIPS // 2))
        sums(both_b, i + 1)
        for n in range(4):
            k = 2 * step_of(i + n // 2) + n % 2

            @pl.when(k != chip)
            def _():
                back_copy(k).start()
        return carry

    lax.fori_loop(0, CHIPS // 4, compute, 0)
    back[chip] = res[chip]

    def get_back(k, carry):
        @pl.when(k != chip)
        def _():
            pltpu.make_async_remote_copy(
                src_ref=res.at[k], dst_ref=back.at[k], send_sem=back_send.at[k], recv_sem=back_recv.at[k],
                device_id={"scene": 2 * k + c}, device_id_type=MESH,
            ).wait()
        return carry

    gives = []
    for n in range(2):
        h = (x // 2 + 1 + n) % 2
        lax.fori_loop(16 * h, 16 * h + 16, get_back, 0)
        for ri in range(2):
            turned[h, ri] = back[pl.ds(16 * h, 16), 8 * ri : 8 * ri + 8, :].reshape(128, 128).T
        give = pltpu.make_async_remote_copy(
            src_ref=turned.at[h, :, pl.ds(pl.multiple_of(64 * other, 64), 64), :], dst_ref=fin.at[h],
            send_sem=fin_send.at[n], recv_sem=fin_recv.at[n], device_id=partner, device_id_type=MESH,
        )
        give.start()
        gives.append(give)
    for h in range(2):
        out_ref[c, :, :, 128 * h : 128 * h + 128] = turned[h, :, pl.ds(pl.multiple_of(64 * c, 64), 64), :]
    for give in gives:
        give.wait()
    for h in range(2):
        out_ref[other, :, :, 128 * h : 128 * h + 128] = fin[h]


def shards(scene_tiles, scene_slot, pair_ref, pair_sec, pair_count):
    pcap = pair_ref.shape[0]
    order = jnp.asarray(feature_order(), BF16)
    vmem = pl.BlockSpec(memory_space=pltpu.VMEM)
    dma = pltpu.SemaphoreType.DMA
    out = pl.pallas_call(
        kernel,
        out_shape=jax.ShapeDtypeStruct((2, 2, pcap, 256), F32),
        in_specs=[pl.BlockSpec(memory_space=pltpu.HBM)] * 6,
        out_specs=vmem,
        scratch_shapes=[
            pltpu.VMEM((320,), jnp.int32),
            pltpu.VMEM((1, 64), jnp.int32),
            pltpu.VMEM((1, 64), jnp.int32),
            pltpu.VMEM((1, 1), jnp.int32),
            pltpu.VMEM((ROWS, 512), BF16),
            pltpu.VMEM(scene_tiles.shape, BF16),
            pltpu.VMEM((AZ, 16, 1024), BF16),
            pltpu.VMEM((2, AZ, 16, 1280), BF16),
            pltpu.VMEM((CHIPS, 16, 128), BF16),
            pltpu.VMEM((2, 16, 128), BF16),
            pltpu.VMEM((512, 512), BF16),
            pltpu.VMEM((CHIPS, 16, 384), BF16),
            pltpu.VMEM((CHIPS, 16, 384), BF16),
            pltpu.VMEM((2, 128), jnp.int32),
            pltpu.VMEM((2, 128), jnp.int32),
            pltpu.VMEM((2, 128), jnp.int32),
            pltpu.VMEM((CHIPS, 2, 128), jnp.int32),
            pltpu.VMEM((512, 128), jnp.int32),
            pltpu.VMEM((CHIPS // 2, 512, 512), BF16),
            pltpu.VMEM((ROWS, 512), BF16),
            pltpu.VMEM((ROWS, 512), F32),
            pltpu.VMEM((ROWS, 512), F32),
            pltpu.VMEM((CHIPS, 16, 128), F32),
            pltpu.VMEM((CHIPS, 16, 128), F32),
            pltpu.VMEM((2, 2, 128, 128), F32),
            pltpu.VMEM((2, 2, 64, 128), F32),
            dma((6,)), dma((2,)), dma((2,)), dma((2,)), dma((CHIPS,)), dma((CHIPS,)), dma((CHIPS,)),
            dma((CHIPS,)), dma((CHIPS,)), dma((CHIPS,)), dma((CHIPS,)), dma((2,)), dma((2,)),
        ],
        compiler_params=pltpu.CompilerParams(
            collective_id=0, has_side_effects=True, vmem_limit_bytes=54 << 20
        ),
        name="coherence",
    )(scene_tiles, scene_slot, pair_ref.reshape(1, pcap), pair_sec.reshape(1, pcap), pair_count.reshape(1, 1), order)
    return out.transpose(2, 0, 1, 3)


def solution(mesh):
    placed = (P("scene", None, None, "strip"), P(), P("scene"), P("scene"), P("scene"))
    return jax.shard_map(
        shards,
        mesh=mesh,
        in_specs=placed,
        out_specs=P("scene", None, None, "strip"),
        check_vma=False,
    )
```

```python
import functools

import jax
import jax.numpy as jnp
import numpy as np
from jax import lax
from jax.experimental import pallas as pl
from jax.experimental.pallas import tpu as pltpu
from jax.sharding import PartitionSpec as P

MESH = pl.DeviceIdType.MESH
F32 = jnp.float32
BF16 = jnp.bfloat16

XS, ZS, CHIPS = 4, 8, 32
STRIPS = 4
SLOTS = 6
AZ = 5
TILES = 8
ROWS = 480


def feature_order():
    order = np.zeros((ROWS, 512), np.float32)
    for az in range(AZ):
        for ri in range(2):
            for cell in range(-10, 38):
                block, w = (cell + 2) // 4, (cell + 2) % 4
                base = 96 * az + 48 * ri
                if 0 <= block < 8:
                    row = base + 8 * w + block
                else:
                    row = base + 32 + 4 * w + {-2: 0, -1: 1, 8: 2, 9: 3}[block]
                if 0 <= cell < 32:
                    lane = 32 * (2 * az + ri) + cell
                else:
                    h = cell + 10 if cell < 0 else cell - 22
                    lane = 32 * (10 + az) + 16 * ri + h
                order[row, lane] = 1.0
    return order


def far_first(i):
    return jnp.where(i == 0, 2, jnp.where(i == 1, 1, jnp.where(i == 2, 3, 0)))


def across(x, i):
    low = lax.rem(x, 2)
    high = x // 2
    flip = jnp.where(lax.rem(i, 3) == 0, low, 1 - low)
    return jnp.where(i < 2, 1 - high, high) * 2 + flip


def along(z, j):
    step = (j + 1) // 2
    return lax.rem(z + jnp.where(lax.rem(j, 2) == 0, ZS // 2 + step, ZS // 2 - step), ZS)


def both_parts(v):
    rows = jnp.zeros((2, v.shape[-1]), F32)
    v = v.astype(F32)
    return jnp.concatenate([v[:, 0, :], rows, v[:, 1, :], rows], axis=0).astype(BF16)


def windows(main, halo):
    row = lax.broadcasted_iota(jnp.int32, main.shape, 0)
    total = main + jnp.where(row < 1, pltpu.roll(halo, 7, 0), pltpu.roll(main, 1, 0))
    total += jnp.where(row < 2, halo, pltpu.roll(main, 2, 0))
    total += jnp.where(row >= 7, pltpu.roll(halo, 1, 0), pltpu.roll(main, 7, 0))
    total += jnp.where(row >= 6, halo, pltpu.roll(main, 6, 0))
    return total


def kernel(
    tiles_hbm, slot_hbm, ref_hbm, sec_hbm, count_hbm, order_hbm, out_ref,
    slot_ref, ref_ref, sec_ref, count_ref, order_ref, raw, ext, edge, edge_par, edge_msg, sent, msg, land, par,
    own_list, lists, lists_par, scene_k, hot, feat, both_a, both_b,
    res, back, turned, fin,
    in_sem, core_send, core_recv, hand_send, hand_recv, edge_send, edge_recv, list_send, list_recv,
    data_send, data_recv, back_send, back_recv, fin_send, fin_recv,
):
    me = lax.axis_index("scene")
    y = lax.axis_index("strip")
    chip, c = me // 2, lax.rem(me, 2)
    other = 1 - c
    x, z = chip // ZS, lax.rem(chip, ZS)
    partner = {"scene": chip * 2 + other}

    barrier = pltpu.get_barrier_semaphore()

    def greet(k, carry):
        @pl.when(k != chip)
        def _():
            pl.semaphore_signal(barrier, inc=1, device_id={"scene": 2 * k + c}, device_id_type=MESH)
        return carry

    pl.semaphore_signal(barrier, inc=1, device_id=partner, device_id_type=MESH)
    lax.fori_loop(0, CHIPS, greet, 0)

    at_left = (chip == 0) & (y > 0)
    at_right = (chip == CHIPS - 1) & (y < STRIPS - 1)
    side = jnp.where(chip == 0, y - 1, y + 1)

    def greet_side(k, carry):
        pl.semaphore_signal(
            barrier, inc=1, device_id={"scene": 2 * k + c, "strip": side}, device_id_type=MESH
        )
        return carry

    @pl.when(at_left | at_right)
    def _():
        lax.fori_loop(0, CHIPS, greet_side, 0)

    gets = [
        pltpu.make_async_copy(src, dst, in_sem.at[n])
        for n, (src, dst) in enumerate((
            (tiles_hbm, raw), (ref_hbm, ref_ref), (sec_hbm, sec_ref), (count_hbm, count_ref),
            (slot_hbm, slot_ref), (order_hbm, order_ref),
        ))
    ]
    for get in gets:
        get.start()
    for get in gets[1:4]:
        get.wait()
    mine = lax.broadcasted_iota(jnp.int32, (1, 64), 1) < count_ref[...]
    for n, ref in enumerate((ref_ref, sec_ref)):
        pair = jnp.where(mine, ref[...], -2)
        own_list[n : n + 1, 0:64] = pair
        own_list[n : n + 1, 64:128] = pair
    ext[:, :, :, 0:128] = jnp.zeros((2, AZ, 16, 128), BF16)
    ext[:, :, :, 1152:1280] = jnp.zeros((2, AZ, 16, 128), BF16)
    gets[0].wait()

    def lines(az, carry):
        for line in range(2):
            ext[line, az, :, 128:1152] = both_parts(raw[:, AZ * line + az])
        return carry

    lax.fori_loop(0, AZ, lines, 0)

    lanes = lax.broadcasted_iota(jnp.int32, (16, 128), 1)
    in32 = lax.rem(lanes, 32)
    row8 = lax.broadcasted_iota(jnp.int32, (2, 8, 128), 1)

    def pack(t, carry):
        at = pl.ds(pl.multiple_of(t * 128, 128), 384)
        groups, halos = [], []
        for az in range(AZ):
            v = [ext[line, az, :, at].astype(F32) for line in range(2)]
            re = jnp.concatenate([v[0][0:8], v[1][0:8]], axis=0)
            im = jnp.concatenate([v[0][8:16], v[1][8:16]], axis=0)
            groups += [re[:, 128:256], im[:, 128:256]]
            near = jnp.where(in32 < 10, pltpu.roll(re, 10, 1)[:, 128:256], pltpu.roll(re, 384 - 22, 1)[:, 128:256])
            far = jnp.where(in32 < 26, pltpu.roll(im, 26, 1)[:, 128:256], pltpu.roll(im, 384 - 6, 1)[:, 128:256])
            halos.append(jnp.where(in32 < 16, near, far))
        groups += halos + [jnp.zeros((16, 128), F32)]
        turned4 = []
        for s in range(4):
            g = groups[4 * s : 4 * s + 4]
            low = lanes < 64
            for a, b in ((0, 2), (1, 3)):
                ga, gb = g[a], g[b]
                g[a] = jnp.where(low, ga, pltpu.roll(gb, 64, 1))
                g[b] = jnp.where(low, pltpu.roll(ga, 64, 1), gb)
            low = lax.rem(lanes, 64) < 32
            for a, b in ((0, 1), (2, 3)):
                ga, gb = g[a], g[b]
                g[a] = jnp.where(low, ga, pltpu.roll(gb, 32, 1))
                g[b] = jnp.where(low, pltpu.roll(ga, 96, 1), gb)
            turned4.append(g)
        for sub in range(4):
            k = 4 * t + sub
            last = turned4[3][sub].reshape(2, 8, 128)
            for s in range(3):
                tile = turned4[s][sub].reshape(2, 8, 128)
                tile = jnp.where(row8 >= 6, pltpu.roll(last, 6 - 2 * s, 1), tile)
                msg[k, :, 128 * s : 128 * s + 128] = tile.reshape(16, 128).astype(BF16)
        return carry

    lax.fori_loop(0, TILES, pack, 0)
    land[chip] = msg[chip]

    def edge_pack(n, start):
        whole = jnp.zeros((16, 128), F32)
        for az in range(AZ):
            v = [ext[line, az, :, start : start + 128].astype(F32) for line in range(2)]
            re = jnp.concatenate([v[0][0:8], v[1][0:8]], axis=0)
            im = jnp.concatenate([v[0][8:16], v[1][8:16]], axis=0)
            for s in range(3 if az == 4 else 1):
                to = 32 * s if az == 4 else 32 * ((az + 2) % 4)
                here = jnp.where(in32 < 16, pltpu.roll(re, 10 + to, 1), pltpu.roll(im, (26 + to) % 128, 1))
                if az == 4:
                    here = pltpu.roll(here.reshape(2, 8, 128), 6 - 2 * s, 1).reshape(16, 128)
                    keep = (lanes // 32 == s) & (row8.reshape(16, 128) >= 6)
                else:
                    keep = lanes // 32 == to // 32
                whole = jnp.where(keep, here, whole)
        edge_msg[n] = whole.astype(BF16)

    def edge_copy(n, to, row):
        return pltpu.make_async_remote_copy(
            src_ref=edge_msg.at[n], dst_ref=edge.at[chip], send_sem=edge_send.at[n], recv_sem=edge_recv,
            device_id={"scene": 2 * to + c, "strip": row}, device_id_type=MESH,
        )

    edge_pack(0, 1024)
    edge_pack(1, 128)
    sides = jnp.where(y < STRIPS - 1, 1, 0) + jnp.where(y > 0, 1, 0)
    pl.semaphore_wait(barrier, CHIPS + sides)

    @pl.when(y < STRIPS - 1)
    def _():
        edge_copy(0, 0, y + 1).start()

    @pl.when(y > 0)
    def _():
        edge_copy(1, CHIPS - 1, y - 1).start()

    order = [across(x, i // ZS) * ZS + along(z, i % ZS) for i in range(CHIPS - 1)]

    def data_copy(i, src, dst, to):
        return pltpu.make_async_remote_copy(
            src_ref=src, dst_ref=dst, send_sem=data_send, recv_sem=data_recv.at[i],
            device_id={"scene": 2 * to + c}, device_id_type=MESH,
        )

    def list_copy(src, dst, to):
        return pltpu.make_async_remote_copy(
            src_ref=src, dst_ref=dst, send_sem=list_send, recv_sem=list_recv,
            device_id={"scene": 2 * to + c}, device_id_type=MESH,
        )

    for i in range(ZS):
        data_copy(i // ZS, msg.at[order[i]], land.at[chip], order[i]).start()
    for i in range(CHIPS - 1):
        list_copy(own_list, lists.at[chip], order[i]).start()
    for i in range(ZS, CHIPS - 1):
        data_copy(i // ZS, msg.at[order[i]], land.at[chip], order[i]).start()

    gets[4].wait()
    gets[5].wait()

    rows = lax.broadcasted_iota(jnp.int32, (512, 320), 0)
    place = lax.rem(rows, 8)
    slot = (rows // 16) * 12 + (lax.rem(rows, 16) // 8) * 6 + place
    slot = jnp.where(place < SLOTS, slot, -7)
    lane = lax.broadcasted_iota(jnp.int32, (512, 320), 1).astype(F32)
    scene = jnp.sum(jnp.where(slot == slot_ref[...].reshape(1, 320), lane + 1.0, 0.0), axis=1, keepdims=True) - 1.0
    scene_k[...] = jnp.broadcast_to(scene, (512, 128)).astype(jnp.int32)

    lists[chip] = own_list[...]

    def hand(i):
        first = across(x, i) * ZS
        many = ZS if i < XS - 1 else ZS - 1
        data_copy(i, msg.at[pl.ds(0, many)], land.at[pl.ds(first, many)], chip).wait_recv()
        copy = pltpu.make_async_remote_copy(
            src_ref=land.at[pl.ds(first, ZS)], dst_ref=par.at[pl.ds(first, ZS)],
            send_sem=hand_send.at[i], recv_sem=hand_recv.at[i], device_id=partner, device_id_type=MESH,
        )
        copy.start()
        return copy

    most = pl.ds(0, CHIPS - 1)
    list_copy(lists.at[most], lists.at[most], chip).wait_recv()
    hand_list = pltpu.make_async_remote_copy(
        src_ref=lists, dst_ref=lists_par, send_sem=core_send.at[0], recv_sem=core_recv.at[0],
        device_id=partner, device_id_type=MESH,
    )
    hand_list.start()
    hands = [hand(0)]
    hand_list.wait()

    half = lax.broadcasted_iota(jnp.int32, (2, 128), 1) // 64

    def one_hot(m, carry):
        for n in range(2):
            pair = jnp.where(half == c, lists[2 * m + n], lists_par[2 * m + n])
            for part in range(2):
                hit = jnp.where(scene_k[...] == pair[part : part + 1, :], 1.0, 0.0).astype(BF16)
                hot[m, :, 256 * part + 128 * n : 256 * part + 128 * n + 128] = hit
        return carry

    lax.fori_loop(0, CHIPS // 2, one_hot, 0)
    hands.append(hand(1))
    hand_edge = pltpu.make_async_remote_copy(
        src_ref=edge, dst_ref=edge_par, send_sem=core_send.at[1], recv_sem=core_recv.at[1],
        device_id=partner, device_id_type=MESH,
    )

    @pl.when(at_left | at_right)
    def _():
        pltpu.make_async_remote_copy(
            src_ref=edge, dst_ref=edge, send_sem=edge_send.at[0], recv_sem=edge_recv,
            device_id={"scene": 2 * chip + c, "strip": side}, device_id_type=MESH,
        ).wait_recv()
        hand_edge.start()

    hands.append(hand(2))
    hands.append(hand(3))
    for copy in hands:
        copy.wait()

    def line_of(mine, others):
        a, b = (v.astype(F32).reshape(CHIPS, 2, 8, 128) for v in (mine, others))
        a = jnp.where(c == 0, a[:, 0], a[:, 1])
        b = jnp.where(c == 0, b[:, 0], b[:, 1])
        pair = [jnp.where(c == 0, a, b), jnp.where(c == 0, b, a)]
        return jnp.stack(pair, axis=1).reshape(64, 8, 128)

    wide = [line_of(*(r[:, :, 128 * s : 128 * s + 128] for r in (land, par))) for s in range(3)]
    part = [v.reshape(512, 128).astype(BF16) for v in wide]
    row = lax.broadcasted_iota(jnp.int32, (64, 8, 128), 1)
    last = jnp.where(
        row < 2, pltpu.roll(wide[0], 2, 1), jnp.where(row < 4, pltpu.roll(wide[1], 4, 1), pltpu.roll(wide[2], 6, 1))
    )
    sent[...] = jnp.concatenate(part + [last.reshape(512, 128).astype(BF16)], axis=1)

    @pl.when(at_left | at_right)
    def _():
        hand_edge.wait()
        lane = lax.broadcasted_iota(jnp.int32, (512, 128), 1)
        left = jnp.where(chip == 0, 1, 0)
        ours = jnp.where(lax.rem(lane, 16) < 10, left, 1 - left) == 1
        fold = line_of(edge[...], edge_par[...])
        got = fold.reshape(512, 128)
        deep = [pltpu.roll(fold, 2 * s + 2, 1).reshape(512, 128) for s in range(3)]
        deep = [pltpu.roll(deep[s], 64 - 32 * s, 1) for s in range(3)]
        level = row.reshape(512, 128)
        deep = jnp.where(level < 2, deep[0], jnp.where(level < 4, deep[1], deep[2]))
        third, fourth = sent[:, 256:384].astype(F32), sent[:, 384:512].astype(F32)
        sent[:, 256:384] = jnp.where(ours & (lane >= 64), got, third).astype(BF16)
        sent[:, 384:512] = jnp.where(ours, jnp.where(lane < 64, got, deep), fourth).astype(BF16)

    feat[...] = lax.dot_general(
        order_ref[...], sent[...], (((1,), (1,)), ((), ())), preferred_element_type=F32
    ).astype(BF16)

    def back_copy(i, src, dst, to):
        return pltpu.make_async_remote_copy(
            src_ref=src, dst_ref=dst, send_sem=back_send, recv_sem=back_recv.at[i],
            device_id={"scene": 2 * to + c}, device_id_type=MESH,
        )

    def step_of(i):
        zp = lax.rem(z // 2 + far_first(lax.rem(i, 4)), 4)
        return across(x, i // 4) * 4 + zp

    def gather(ref, i):
        ref[...] = jnp.dot(feat[...], hot[step_of(i)], preferred_element_type=F32)

    def sums(ref, i):
        main, halo = [0.0] * 4, [0.0] * 4
        for az in range(AZ):
            a0, b0 = ref[96 * az : 96 * az + 48, 0:256], ref[96 * az : 96 * az + 48, 256:512]
            a1, b1 = ref[96 * az + 48 : 96 * az + 96, 0:256], ref[96 * az + 48 : 96 * az + 96, 256:512]
            planes = (a0 * b0 + a1 * b1, a1 * b0 - a0 * b1, a0 * a0 + a1 * a1, b0 * b0 + b1 * b1)
            for n, plane in enumerate(planes):
                for w in range(4):
                    main[n] = main[n] + plane[8 * w : 8 * w + 8]
                for w in range(4, 6):
                    halo[n] = halo[n] + plane[8 * w : 8 * w + 8]
        looks = [windows(u, v + pltpu.roll(v, 4, 0)) for u, v in zip(main, halo)]
        scale = lax.rsqrt(looks[2] * looks[3] + 1e-06)
        value = jnp.concatenate([looks[0] * scale, looks[1] * scale], axis=0)
        k = 2 * step_of(i)
        res[k] = value[:, 0:128]
        res[k + 1] = value[:, 128:256]

    gather(both_a, 0)

    def compute(j, carry):
        i = 2 * j
        gather(both_b, i + 1)
        sums(both_a, i)
        gather(both_a, lax.rem(i + 2, CHIPS // 2))
        sums(both_b, i + 1)
        for n in range(4):
            k = 2 * step_of(i + n // 2) + n % 2

            @pl.when(k != chip)
            def _():
                back_copy(j // 2, res.at[k], back.at[chip], k).start()
        return carry

    lax.fori_loop(0, CHIPS // 4, compute, 0)
    back[chip] = res[chip]

    gives = []
    for n in range(2):
        h = (x // 2 + 1 + n) % 2
        for i in (2 * n, 2 * n + 1):
            some = pl.ds(0, ZS if i < XS - 1 else ZS - 1)
            back_copy(i, res.at[some], back.at[some], chip).wait_recv()
        for ri in range(2):
            turned[h, ri] = back[pl.ds(16 * h, 16), 8 * ri : 8 * ri + 8, :].reshape(128, 128).T
        give = pltpu.make_async_remote_copy(
            src_ref=turned.at[h, :, pl.ds(pl.multiple_of(64 * other, 64), 64), :], dst_ref=fin.at[h],
            send_sem=fin_send.at[n], recv_sem=fin_recv.at[n], device_id=partner, device_id_type=MESH,
        )
        give.start()
        gives.append(give)
    for h in range(2):
        out_ref[c, :, :, 128 * h : 128 * h + 128] = turned[h, :, pl.ds(pl.multiple_of(64 * c, 64), 64), :]
    for give in gives:
        give.wait()
    for h in range(2):
        out_ref[other, :, :, 128 * h : 128 * h + 128] = fin[h]

    @pl.when(y < STRIPS - 1)
    def _():
        edge_copy(0, 0, y + 1).wait_send()

    @pl.when(y > 0)
    def _():
        edge_copy(1, CHIPS - 1, y - 1).wait_send()

    list_copy(lists.at[most], lists.at[most], chip).wait_send()
    data_copy(0, msg.at[most], land.at[most], chip).wait_send()
    back_copy(0, res.at[most], back.at[most], chip).wait_send()


def shards(scene_tiles, scene_slot, pair_ref, pair_sec, pair_count):
    pcap = pair_ref.shape[0]
    order = jnp.asarray(feature_order(), BF16)
    vmem = pl.BlockSpec(memory_space=pltpu.VMEM)
    dma = pltpu.SemaphoreType.DMA
    out = pl.pallas_call(
        kernel,
        out_shape=jax.ShapeDtypeStruct((2, 2, pcap, 256), F32),
        in_specs=[pl.BlockSpec(memory_space=pltpu.HBM)] * 6,
        out_specs=vmem,
        scratch_shapes=[
            pltpu.VMEM((320,), jnp.int32),
            pltpu.VMEM((1, 64), jnp.int32),
            pltpu.VMEM((1, 64), jnp.int32),
            pltpu.VMEM((1, 1), jnp.int32),
            pltpu.VMEM((ROWS, 512), BF16),
            pltpu.VMEM(scene_tiles.shape, BF16),
            pltpu.VMEM((2, AZ, 16, 1280), BF16),
            pltpu.VMEM((CHIPS, 16, 128), BF16),
            pltpu.VMEM((CHIPS, 16, 128), BF16),
            pltpu.VMEM((2, 16, 128), BF16),
            pltpu.VMEM((512, 512), BF16),
            pltpu.VMEM((CHIPS, 16, 384), BF16),
            pltpu.VMEM((CHIPS, 16, 384), BF16),
            pltpu.VMEM((CHIPS, 16, 384), BF16),
            pltpu.VMEM((2, 128), jnp.int32),
            pltpu.VMEM((CHIPS, 2, 128), jnp.int32),
            pltpu.VMEM((CHIPS, 2, 128), jnp.int32),
            pltpu.VMEM((512, 128), jnp.int32),
            pltpu.VMEM((CHIPS // 2, 512, 512), BF16),
            pltpu.VMEM((ROWS, 512), BF16),
            pltpu.VMEM((ROWS, 512), F32),
            pltpu.VMEM((ROWS, 512), F32),
            pltpu.VMEM((CHIPS, 16, 128), F32),
            pltpu.VMEM((CHIPS, 16, 128), F32),
            pltpu.VMEM((2, 2, 128, 128), F32),
            pltpu.VMEM((2, 2, 64, 128), F32),
            dma((6,)), dma((2,)), dma((2,)), dma((XS,)), dma((XS,)), dma((2,)), dma, dma, dma,
            dma, dma((XS,)), dma, dma((XS,)), dma((2,)), dma((2,)),
        ],
        compiler_params=pltpu.CompilerParams(
            collective_id=0, has_side_effects=True, vmem_limit_bytes=54 << 20
        ),
        name="coherence",
    )(scene_tiles, scene_slot, pair_ref.reshape(1, pcap), pair_sec.reshape(1, pcap), pair_count.reshape(1, 1), order)
    return out.transpose(2, 0, 1, 3)


def solution(mesh):
    placed = (P("scene", None, None, "strip"), P(), P("scene"), P("scene"), P("scene"))
    return jax.shard_map(
        shards,
        mesh=mesh,
        in_specs=placed,
        out_specs=P("scene", None, None, "strip"),
        check_vma=False,
    )
```

```python
import functools

import jax
import jax.numpy as jnp
import numpy as np
from jax import lax
from jax.experimental import pallas as pl
from jax.experimental.pallas import tpu as pltpu
from jax.sharding import PartitionSpec as P

MESH = pl.DeviceIdType.MESH
F32 = jnp.float32
BF16 = jnp.bfloat16

XS, ZS, CHIPS = 4, 8, 32
STRIPS = 4
SLOTS = 6
AZ = 5
TILES = 8
ROWS = 480


def feature_order():
    order = np.zeros((ROWS, 512), np.float32)
    for az in range(AZ):
        for ri in range(2):
            for cell in range(-10, 38):
                block, w = (cell + 2) // 4, (cell + 2) % 4
                base = 96 * az + 48 * ri
                if 0 <= block < 8:
                    row = base + 8 * w + block
                else:
                    row = base + 32 + 4 * w + {-2: 0, -1: 1, 8: 2, 9: 3}[block]
                if 0 <= cell < 32:
                    lane = 32 * (2 * az + ri) + cell
                else:
                    h = cell + 10 if cell < 0 else cell - 22
                    lane = 32 * (10 + az) + 16 * ri + h
                order[row, lane] = 1.0
    return order


def far_first(i):
    return jnp.where(i == 0, 2, jnp.where(i == 1, 1, jnp.where(i == 2, 3, 0)))


def across(x, i):
    low = lax.rem(x, 2)
    high = x // 2
    flip = jnp.where(lax.rem(i, 3) == 0, low, 1 - low)
    return jnp.where(i < 2, 1 - high, high) * 2 + flip


def along(z, j):
    step = (j + 1) // 2
    return lax.rem(z + jnp.where(lax.rem(j, 2) == 0, ZS // 2 + step, ZS // 2 - step), ZS)


def both_parts(v):
    rows = jnp.zeros((2, v.shape[-1]), F32)
    v = v.astype(F32)
    return jnp.concatenate([v[:, 0, :], rows, v[:, 1, :], rows], axis=0).astype(BF16)


def windows(main, halo):
    row = lax.broadcasted_iota(jnp.int32, main.shape, 0)
    total = main + jnp.where(row < 1, pltpu.roll(halo, 7, 0), pltpu.roll(main, 1, 0))
    total += jnp.where(row < 2, halo, pltpu.roll(main, 2, 0))
    total += jnp.where(row >= 7, pltpu.roll(halo, 1, 0), pltpu.roll(main, 7, 0))
    total += jnp.where(row >= 6, halo, pltpu.roll(main, 6, 0))
    return total


def kernel(
    tiles_hbm, slot_hbm, ref_hbm, sec_hbm, count_hbm, order_hbm, out_ref,
    slot_ref, ref_ref, sec_ref, count_ref, order_ref, raw, ext, edge, edge_par, edge_msg, sent, msg, land, par,
    own_list, lists, lists_par, scene_k, hot, feat, both_a, both_b,
    res, back, turned, fin,
    in_sem, core_send, core_recv, hand_send, hand_recv, edge_send, edge_recv, list_send, list_recv,
    data_send, data_recv, back_send, back_recv, fin_send, fin_recv,
):
    me = lax.axis_index("scene")
    y = lax.axis_index("strip")
    chip, c = me // 2, lax.rem(me, 2)
    other = 1 - c
    x, z = chip // ZS, lax.rem(chip, ZS)
    partner = {"scene": chip * 2 + other}

    barrier = pltpu.get_barrier_semaphore()

    def greet(k, carry):
        @pl.when(k != chip)
        def _():
            pl.semaphore_signal(barrier, inc=1, device_id={"scene": 2 * k + c}, device_id_type=MESH)
        return carry

    pl.semaphore_signal(barrier, inc=1, device_id=partner, device_id_type=MESH)
    lax.fori_loop(0, CHIPS, greet, 0)

    at_left = (chip == 0) & (y > 0)
    at_right = (chip == CHIPS - 1) & (y < STRIPS - 1)
    side = jnp.where(chip == 0, y - 1, y + 1)

    def greet_side(k, carry):
        pl.semaphore_signal(
            barrier, inc=1, device_id={"scene": 2 * k + c, "strip": side}, device_id_type=MESH
        )
        return carry

    @pl.when(at_left | at_right)
    def _():
        lax.fori_loop(0, CHIPS, greet_side, 0)

    gets = [
        pltpu.make_async_copy(src, dst, in_sem.at[n])
        for n, (src, dst) in enumerate((
            (tiles_hbm, raw), (ref_hbm, ref_ref), (sec_hbm, sec_ref), (count_hbm, count_ref),
            (slot_hbm, slot_ref), (order_hbm, order_ref),
        ))
    ]
    for get in gets:
        get.start()
    for get in gets[1:4]:
        get.wait()
    mine = lax.broadcasted_iota(jnp.int32, (1, 64), 1) < count_ref[...]
    for n, ref in enumerate((ref_ref, sec_ref)):
        pair = jnp.where(mine, ref[...], -2)
        own_list[n : n + 1, 0:64] = pair
        own_list[n : n + 1, 64:128] = pair
    ext[:, :, :, 0:128] = jnp.zeros((2, AZ, 16, 128), BF16)
    ext[:, :, :, 1152:1280] = jnp.zeros((2, AZ, 16, 128), BF16)
    gets[0].wait()

    def lines(az, carry):
        for line in range(2):
            ext[line, az, :, 128:1152] = both_parts(raw[:, AZ * line + az])
        return carry

    lax.fori_loop(0, AZ, lines, 0)

    lanes = lax.broadcasted_iota(jnp.int32, (16, 128), 1)
    in32 = lax.rem(lanes, 32)
    row8 = lax.broadcasted_iota(jnp.int32, (2, 8, 128), 1)

    def pack(t, carry):
        at = pl.ds(pl.multiple_of(t * 128, 128), 384)
        groups, halos = [], []
        for az in range(AZ):
            v = [ext[line, az, :, at].astype(F32) for line in range(2)]
            re = jnp.concatenate([v[0][0:8], v[1][0:8]], axis=0)
            im = jnp.concatenate([v[0][8:16], v[1][8:16]], axis=0)
            groups += [re[:, 128:256], im[:, 128:256]]
            near = jnp.where(in32 < 10, pltpu.roll(re, 10, 1)[:, 128:256], pltpu.roll(re, 384 - 22, 1)[:, 128:256])
            far = jnp.where(in32 < 26, pltpu.roll(im, 26, 1)[:, 128:256], pltpu.roll(im, 384 - 6, 1)[:, 128:256])
            halos.append(jnp.where(in32 < 16, near, far))
        groups += halos + [jnp.zeros((16, 128), F32)]
        turned4 = []
        for s in range(4):
            g = groups[4 * s : 4 * s + 4]
            low = lanes < 64
            for a, b in ((0, 2), (1, 3)):
                ga, gb = g[a], g[b]
                g[a] = jnp.where(low, ga, pltpu.roll(gb, 64, 1))
                g[b] = jnp.where(low, pltpu.roll(ga, 64, 1), gb)
            low = lax.rem(lanes, 64) < 32
            for a, b in ((0, 1), (2, 3)):
                ga, gb = g[a], g[b]
                g[a] = jnp.where(low, ga, pltpu.roll(gb, 32, 1))
                g[b] = jnp.where(low, pltpu.roll(ga, 96, 1), gb)
            turned4.append(g)
        for sub in range(4):
            k = 4 * t + sub
            last = turned4[3][sub].reshape(2, 8, 128)
            for s in range(3):
                tile = turned4[s][sub].reshape(2, 8, 128)
                tile = jnp.where(row8 >= 6, pltpu.roll(last, 6 - 2 * s, 1), tile)
                msg[k, :, 128 * s : 128 * s + 128] = tile.reshape(16, 128).astype(BF16)
        return carry

    lax.fori_loop(0, TILES, pack, 0)
    land[chip] = msg[chip]

    def edge_pack(n, start):
        whole = jnp.zeros((16, 128), F32)
        for az in range(AZ):
            v = [ext[line, az, :, start : start + 128].astype(F32) for line in range(2)]
            re = jnp.concatenate([v[0][0:8], v[1][0:8]], axis=0)
            im = jnp.concatenate([v[0][8:16], v[1][8:16]], axis=0)
            for s in range(3 if az == 4 else 1):
                to = 32 * s if az == 4 else 32 * ((az + 2) % 4)
                here = jnp.where(in32 < 16, pltpu.roll(re, 10 + to, 1), pltpu.roll(im, (26 + to) % 128, 1))
                if az == 4:
                    here = pltpu.roll(here.reshape(2, 8, 128), 6 - 2 * s, 1).reshape(16, 128)
                    keep = (lanes // 32 == s) & (row8.reshape(16, 128) >= 6)
                else:
                    keep = lanes // 32 == to // 32
                whole = jnp.where(keep, here, whole)
        edge_msg[n] = whole.astype(BF16)

    def edge_copy(n, to, row):
        return pltpu.make_async_remote_copy(
            src_ref=edge_msg.at[n], dst_ref=edge.at[chip], send_sem=edge_send.at[n], recv_sem=edge_recv,
            device_id={"scene": 2 * to + c, "strip": row}, device_id_type=MESH,
        )

    edge_pack(0, 1024)
    edge_pack(1, 128)
    sides = jnp.where(y < STRIPS - 1, 1, 0) + jnp.where(y > 0, 1, 0)
    pl.semaphore_wait(barrier, CHIPS + sides)

    @pl.when(y < STRIPS - 1)
    def _():
        edge_copy(0, 0, y + 1).start()

    @pl.when(y > 0)
    def _():
        edge_copy(1, CHIPS - 1, y - 1).start()

    order = [across(x, i // ZS) * ZS + along(z, i % ZS) for i in range(CHIPS - 1)]

    def data_copy(i, src, dst, to):
        return pltpu.make_async_remote_copy(
            src_ref=src, dst_ref=dst, send_sem=data_send, recv_sem=data_recv.at[i],
            device_id={"scene": 2 * to + c}, device_id_type=MESH,
        )

    def list_copy(src, dst, to):
        return pltpu.make_async_remote_copy(
            src_ref=src, dst_ref=dst, send_sem=list_send, recv_sem=list_recv,
            device_id={"scene": 2 * to + c}, device_id_type=MESH,
        )

    for i in range(ZS):
        data_copy(i // ZS, msg.at[order[i]], land.at[chip], order[i]).start()
    for i in range(CHIPS - 1):
        list_copy(own_list, lists.at[chip], order[i]).start()
    for i in range(ZS, CHIPS - 1):
        data_copy(i // ZS, msg.at[order[i]], land.at[chip], order[i]).start()

    gets[4].wait()
    gets[5].wait()

    rows = lax.broadcasted_iota(jnp.int32, (512, 320), 0)
    place = lax.rem(rows, 8)
    slot = (rows // 16) * 12 + (lax.rem(rows, 16) // 8) * 6 + place
    slot = jnp.where(place < SLOTS, slot, -7)
    lane = lax.broadcasted_iota(jnp.int32, (512, 320), 1).astype(F32)
    scene = jnp.sum(jnp.where(slot == slot_ref[...].reshape(1, 320), lane + 1.0, 0.0), axis=1, keepdims=True) - 1.0
    scene_k[...] = jnp.broadcast_to(scene, (512, 128)).astype(jnp.int32)

    lists[chip] = own_list[...]

    def hand(i):
        first = across(x, i) * ZS
        many = ZS if i < XS - 1 else ZS - 1
        data_copy(i, msg.at[pl.ds(0, many)], land.at[pl.ds(first, many)], chip).wait_recv()
        copy = pltpu.make_async_remote_copy(
            src_ref=land.at[pl.ds(first, ZS)], dst_ref=par.at[pl.ds(first, ZS)],
            send_sem=hand_send.at[i], recv_sem=hand_recv.at[i], device_id=partner, device_id_type=MESH,
        )
        copy.start()
        return copy

    most = pl.ds(0, CHIPS - 1)
    list_copy(lists.at[most], lists.at[most], chip).wait_recv()
    hand_list = pltpu.make_async_remote_copy(
        src_ref=lists, dst_ref=lists_par, send_sem=core_send.at[0], recv_sem=core_recv.at[0],
        device_id=partner, device_id_type=MESH,
    )
    hand_list.start()
    hands = [hand(0)]
    hand_list.wait()

    half = lax.broadcasted_iota(jnp.int32, (2, 128), 1) // 64

    def one_hot(m, carry):
        for n in range(2):
            pair = jnp.where(half == c, lists[2 * m + n], lists_par[2 * m + n])
            for part in range(2):
                hit = jnp.where(scene_k[...] == pair[part : part + 1, :], 1.0, 0.0).astype(BF16)
                hot[m, :, 256 * part + 128 * n : 256 * part + 128 * n + 128] = hit
        return carry

    lax.fori_loop(0, CHIPS // 2, one_hot, 0)
    hands.append(hand(1))
    hand_edge = pltpu.make_async_remote_copy(
        src_ref=edge, dst_ref=edge_par, send_sem=core_send.at[1], recv_sem=core_recv.at[1],
        device_id=partner, device_id_type=MESH,
    )

    @pl.when(at_left | at_right)
    def _():
        pltpu.make_async_remote_copy(
            src_ref=edge, dst_ref=edge, send_sem=edge_send.at[0], recv_sem=edge_recv,
            device_id={"scene": 2 * chip + c, "strip": side}, device_id_type=MESH,
        ).wait_recv()
        hand_edge.start()

    hands.append(hand(2))
    hands.append(hand(3))
    for copy in hands:
        copy.wait()

    def line_of(mine, others):
        a, b = (v.astype(F32).reshape(CHIPS, 2, 8, 128) for v in (mine, others))
        a = jnp.where(c == 0, a[:, 0], a[:, 1])
        b = jnp.where(c == 0, b[:, 0], b[:, 1])
        pair = [jnp.where(c == 0, a, b), jnp.where(c == 0, b, a)]
        return jnp.stack(pair, axis=1).reshape(64, 8, 128)

    wide = [line_of(*(r[:, :, 128 * s : 128 * s + 128] for r in (land, par))) for s in range(3)]
    part = [v.reshape(512, 128).astype(BF16) for v in wide]
    row = lax.broadcasted_iota(jnp.int32, (64, 8, 128), 1)
    last = jnp.where(
        row < 2, pltpu.roll(wide[0], 2, 1), jnp.where(row < 4, pltpu.roll(wide[1], 4, 1), pltpu.roll(wide[2], 6, 1))
    )
    sent[...] = jnp.concatenate(part + [last.reshape(512, 128).astype(BF16)], axis=1)

    @pl.when(at_left | at_right)
    def _():
        hand_edge.wait()
        lane = lax.broadcasted_iota(jnp.int32, (512, 128), 1)
        left = jnp.where(chip == 0, 1, 0)
        ours = jnp.where(lax.rem(lane, 16) < 10, left, 1 - left) == 1
        fold = line_of(edge[...], edge_par[...])
        got = fold.reshape(512, 128)
        deep = [pltpu.roll(fold, 2 * s + 2, 1).reshape(512, 128) for s in range(3)]
        deep = [pltpu.roll(deep[s], 64 - 32 * s, 1) for s in range(3)]
        level = row.reshape(512, 128)
        deep = jnp.where(level < 2, deep[0], jnp.where(level < 4, deep[1], deep[2]))
        third, fourth = sent[:, 256:384].astype(F32), sent[:, 384:512].astype(F32)
        sent[:, 256:384] = jnp.where(ours & (lane >= 64), got, third).astype(BF16)
        sent[:, 384:512] = jnp.where(ours, jnp.where(lane < 64, got, deep), fourth).astype(BF16)

    feat[...] = lax.dot_general(
        order_ref[...], sent[...], (((1,), (1,)), ((), ())), preferred_element_type=F32
    ).astype(BF16)

    def back_copy(i, src, dst, to):
        return pltpu.make_async_remote_copy(
            src_ref=src, dst_ref=dst, send_sem=back_send, recv_sem=back_recv.at[i],
            device_id={"scene": 2 * to + c}, device_id_type=MESH,
        )

    def step_of(i):
        zp = lax.rem(z // 2 + far_first(lax.rem(i, 4)), 4)
        return across(x, i // 4) * 4 + zp

    def gather(ref, i):
        ref[...] = jnp.dot(feat[...], hot[step_of(i)], preferred_element_type=F32)

    def sums(ref, i):
        main, halo = [0.0] * 4, [0.0] * 4
        for az in range(AZ):
            a0, b0 = ref[96 * az : 96 * az + 48, 0:256], ref[96 * az : 96 * az + 48, 256:512]
            a1, b1 = ref[96 * az + 48 : 96 * az + 96, 0:256], ref[96 * az + 48 : 96 * az + 96, 256:512]
            planes = (a0 * b0 + a1 * b1, a1 * b0 - a0 * b1, a0 * a0 + a1 * a1, b0 * b0 + b1 * b1)
            for n, plane in enumerate(planes):
                for w in range(4):
                    main[n] = main[n] + plane[8 * w : 8 * w + 8]
                for w in range(4, 6):
                    halo[n] = halo[n] + plane[8 * w : 8 * w + 8]
        looks = [windows(u, v + pltpu.roll(v, 4, 0)) for u, v in zip(main, halo)]
        scale = lax.rsqrt(looks[2] * looks[3] + 1e-06)
        value = jnp.concatenate([looks[0] * scale, looks[1] * scale], axis=0)
        k = 2 * step_of(i)
        res[k] = value[:, 0:128]
        res[k + 1] = value[:, 128:256]

    def compute(j, carry):
        i = 2 * j
        gather(both_a, i)
        sums(both_a, i)
        gather(both_b, i + 1)
        sums(both_b, i + 1)
        for n in range(4):
            k = 2 * step_of(i + n // 2) + n % 2

            @pl.when(k != chip)
            def _():
                back_copy(j // 2, res.at[k], back.at[chip], k).start()
        return carry

    lax.fori_loop(0, CHIPS // 4, compute, 0)
    back[chip] = res[chip]

    gives = []
    for n in range(2):
        h = (x // 2 + 1 + n) % 2
        for i in (2 * n, 2 * n + 1):
            some = pl.ds(0, ZS if i < XS - 1 else ZS - 1)
            back_copy(i, res.at[some], back.at[some], chip).wait_recv()
        for ri in range(2):
            turned[h, ri] = back[pl.ds(16 * h, 16), 8 * ri : 8 * ri + 8, :].reshape(128, 128).T
        give = pltpu.make_async_remote_copy(
            src_ref=turned.at[h, :, pl.ds(pl.multiple_of(64 * other, 64), 64), :], dst_ref=fin.at[h],
            send_sem=fin_send.at[n], recv_sem=fin_recv.at[n], device_id=partner, device_id_type=MESH,
        )
        give.start()
        gives.append(give)
    for h in range(2):
        out_ref[c, :, :, 128 * h : 128 * h + 128] = turned[h, :, pl.ds(pl.multiple_of(64 * c, 64), 64), :]
    for give in gives:
        give.wait()
    for h in range(2):
        out_ref[other, :, :, 128 * h : 128 * h + 128] = fin[h]

    @pl.when(y < STRIPS - 1)
    def _():
        edge_copy(0, 0, y + 1).wait_send()

    @pl.when(y > 0)
    def _():
        edge_copy(1, CHIPS - 1, y - 1).wait_send()

    list_copy(lists.at[most], lists.at[most], chip).wait_send()
    data_copy(0, msg.at[most], land.at[most], chip).wait_send()
    back_copy(0, res.at[most], back.at[most], chip).wait_send()


def shards(scene_tiles, scene_slot, pair_ref, pair_sec, pair_count):
    pcap = pair_ref.shape[0]
    order = jnp.asarray(feature_order(), BF16)
    vmem = pl.BlockSpec(memory_space=pltpu.VMEM)
    dma = pltpu.SemaphoreType.DMA
    arrays = (
        scene_tiles, scene_slot, pair_ref.reshape(1, pcap), pair_sec.reshape(1, pcap),
        pair_count.reshape(1, 1), order,
    )
    out = pl.pallas_call(
        kernel,
        out_shape=jax.ShapeDtypeStruct((2, 2, pcap, 256), F32),
        in_specs=[pl.BlockSpec(memory_space=pltpu.HBM)] * 6,
        out_specs=vmem,
        scratch_shapes=[
            pltpu.VMEM((320,), jnp.int32),
            pltpu.VMEM((1, 64), jnp.int32),
            pltpu.VMEM((1, 64), jnp.int32),
            pltpu.VMEM((1, 1), jnp.int32),
            pltpu.VMEM((ROWS, 512), BF16),
            pltpu.VMEM(scene_tiles.shape, BF16),
            pltpu.VMEM((2, AZ, 16, 1280), BF16),
            pltpu.VMEM((CHIPS, 16, 128), BF16),
            pltpu.VMEM((CHIPS, 16, 128), BF16),
            pltpu.VMEM((2, 16, 128), BF16),
            pltpu.VMEM((512, 512), BF16),
            pltpu.VMEM((CHIPS, 16, 384), BF16),
            pltpu.VMEM((CHIPS, 16, 384), BF16),
            pltpu.VMEM((CHIPS, 16, 384), BF16),
            pltpu.VMEM((2, 128), jnp.int32),
            pltpu.VMEM((CHIPS, 2, 128), jnp.int32),
            pltpu.VMEM((CHIPS, 2, 128), jnp.int32),
            pltpu.VMEM((512, 128), jnp.int32),
            pltpu.VMEM((CHIPS // 2, 512, 512), BF16),
            pltpu.VMEM((ROWS, 512), BF16),
            pltpu.VMEM((ROWS, 512), F32),
            pltpu.VMEM((ROWS, 512), F32),
            pltpu.VMEM((CHIPS, 16, 128), F32),
            pltpu.VMEM((CHIPS, 16, 128), F32),
            pltpu.VMEM((2, 2, 128, 128), F32),
            pltpu.VMEM((2, 2, 64, 128), F32),
            dma((6,)), dma((2,)), dma((2,)), dma((XS,)), dma((XS,)), dma((2,)), dma, dma, dma,
            dma, dma((XS,)), dma, dma((XS,)), dma((2,)), dma((2,)),
        ],
        compiler_params=pltpu.CompilerParams(
            collective_id=0, has_side_effects=True, vmem_limit_bytes=40 << 20
        ),
        name="coherence",
    )(*(v if v.size == 1 else pltpu.with_memory_space_constraint(v, pltpu.HBM) for v in arrays))
    return out.transpose(2, 0, 1, 3)


def solution(mesh):
    placed = (P("scene", None, None, "strip"), P(), P("scene"), P("scene"), P("scene"))
    return jax.shard_map(
        shards,
        mesh=mesh,
        in_specs=placed,
        out_specs=P("scene", None, None, "strip"),
        check_vma=False,
    )
```

```python
import functools

import jax
import jax.numpy as jnp
import numpy as np
from jax import lax
from jax.experimental import pallas as pl
from jax.experimental.pallas import tpu as pltpu
from jax.sharding import PartitionSpec as P

MESH = pl.DeviceIdType.MESH
F32 = jnp.float32
BF16 = jnp.bfloat16

XS, ZS, CHIPS = 4, 8, 32
STRIPS = 4
SLOTS = 6
AZ = 5
TILES = 8
ROWS = 480


def feature_order():
    order = np.zeros((ROWS, 512), np.float32)
    for az in range(AZ):
        for ri in range(2):
            for cell in range(-10, 38):
                block, w = (cell + 2) // 4, (cell + 2) % 4
                base = 96 * az + 48 * ri
                if 0 <= block < 8:
                    row = base + 8 * w + block
                else:
                    row = base + 32 + 4 * w + {-2: 0, -1: 1, 8: 2, 9: 3}[block]
                if 0 <= cell < 32:
                    lane = 32 * (2 * az + ri) + cell
                else:
                    h = cell + 10 if cell < 0 else cell - 22
                    lane = 32 * (10 + az) + 16 * ri + h
                order[row, lane] = 1.0
    return order


def far_first(i):
    return jnp.where(i == 0, 2, jnp.where(i == 1, 1, jnp.where(i == 2, 3, 0)))


def across(x, i):
    low = lax.rem(x, 2)
    high = x // 2
    flip = jnp.where(lax.rem(i, 3) == 0, low, 1 - low)
    return jnp.where(i < 2, 1 - high, high) * 2 + flip


def along(z, j):
    step = (j + 1) // 2
    return lax.rem(z + jnp.where(lax.rem(j, 2) == 0, ZS // 2 + step, ZS // 2 - step), ZS)


def both_parts(v):
    rows = jnp.zeros((2, v.shape[-1]), F32)
    v = v.astype(F32)
    return jnp.concatenate([v[:, 0, :], rows, v[:, 1, :], rows], axis=0).astype(BF16)


def windows(main, halo):
    row = lax.broadcasted_iota(jnp.int32, main.shape, 0)
    total = main + jnp.where(row < 1, pltpu.roll(halo, 7, 0), pltpu.roll(main, 1, 0))
    total += jnp.where(row < 2, halo, pltpu.roll(main, 2, 0))
    total += jnp.where(row >= 7, pltpu.roll(halo, 1, 0), pltpu.roll(main, 7, 0))
    total += jnp.where(row >= 6, halo, pltpu.roll(main, 6, 0))
    return total


def kernel(
    tiles_hbm, slot_hbm, ref_hbm, sec_hbm, count_hbm, order_hbm, out_ref,
    slot_ref, ref_ref, sec_ref, count_ref, order_ref, raw, ext, edge, edge_par, edge_msg, sent, msg, land, par,
    own_list, lists, lists_par, scene_k, hot, feat, both_a, both_b,
    res, back, turned, fin,
    in_sem, core_send, core_recv, hand_send, hand_recv, edge_send, edge_recv, list_send, list_recv,
    data_send, data_recv, back_send, back_recv, fin_send, fin_recv,
):
    me = lax.axis_index("scene")
    y = lax.axis_index("strip")
    chip, c = me // 2, lax.rem(me, 2)
    other = 1 - c
    x, z = chip // ZS, lax.rem(chip, ZS)
    partner = {"scene": chip * 2 + other}

    barrier = pltpu.get_barrier_semaphore()

    def greet(k, carry):
        @pl.when(k != chip)
        def _():
            pl.semaphore_signal(barrier, inc=1, device_id={"scene": 2 * k + c}, device_id_type=MESH)
        return carry

    pl.semaphore_signal(barrier, inc=1, device_id=partner, device_id_type=MESH)
    lax.fori_loop(0, CHIPS, greet, 0)

    at_left = (chip == 0) & (y > 0)
    at_right = (chip == CHIPS - 1) & (y < STRIPS - 1)
    side = jnp.where(chip == 0, y - 1, y + 1)

    def greet_side(k, carry):
        pl.semaphore_signal(
            barrier, inc=1, device_id={"scene": 2 * k + c, "strip": side}, device_id_type=MESH
        )
        return carry

    @pl.when(at_left | at_right)
    def _():
        lax.fori_loop(0, CHIPS, greet_side, 0)

    gets = [
        pltpu.make_async_copy(src, dst, in_sem.at[n])
        for n, (src, dst) in enumerate((
            (tiles_hbm, raw), (ref_hbm, ref_ref), (sec_hbm, sec_ref), (count_hbm, count_ref),
            (slot_hbm, slot_ref), (order_hbm, order_ref),
        ))
    ]
    for get in gets:
        get.start()
    for get in gets[1:4]:
        get.wait()
    mine = lax.broadcasted_iota(jnp.int32, (1, 64), 1) < count_ref[...]
    for n, ref in enumerate((ref_ref, sec_ref)):
        pair = jnp.where(mine, ref[...], -2)
        own_list[n : n + 1, 0:64] = pair
        own_list[n : n + 1, 64:128] = pair
    ext[:, :, :, 0:128] = jnp.zeros((2, AZ, 16, 128), BF16)
    ext[:, :, :, 1152:1280] = jnp.zeros((2, AZ, 16, 128), BF16)
    gets[0].wait()

    def lines(az, carry):
        for line in range(2):
            ext[line, az, :, 128:1152] = both_parts(raw[:, AZ * line + az])
        return carry

    lax.fori_loop(0, AZ, lines, 0)

    lanes = lax.broadcasted_iota(jnp.int32, (16, 128), 1)
    in32 = lax.rem(lanes, 32)
    row8 = lax.broadcasted_iota(jnp.int32, (2, 8, 128), 1)

    def pack(t, carry):
        at = pl.ds(pl.multiple_of(t * 128, 128), 384)
        groups, halos = [], []
        for az in range(AZ):
            v = [ext[line, az, :, at].astype(F32) for line in range(2)]
            re = jnp.concatenate([v[0][0:8], v[1][0:8]], axis=0)
            im = jnp.concatenate([v[0][8:16], v[1][8:16]], axis=0)
            groups += [re[:, 128:256], im[:, 128:256]]
            near = jnp.where(in32 < 10, pltpu.roll(re, 10, 1)[:, 128:256], pltpu.roll(re, 384 - 22, 1)[:, 128:256])
            far = jnp.where(in32 < 26, pltpu.roll(im, 26, 1)[:, 128:256], pltpu.roll(im, 384 - 6, 1)[:, 128:256])
            halos.append(jnp.where(in32 < 16, near, far))
        groups += halos + [jnp.zeros((16, 128), F32)]
        turned4 = []
        for s in range(4):
            g = groups[4 * s : 4 * s + 4]
            low = lanes < 64
            for a, b in ((0, 2), (1, 3)):
                ga, gb = g[a], g[b]
                g[a] = jnp.where(low, ga, pltpu.roll(gb, 64, 1))
                g[b] = jnp.where(low, pltpu.roll(ga, 64, 1), gb)
            low = lax.rem(lanes, 64) < 32
            for a, b in ((0, 1), (2, 3)):
                ga, gb = g[a], g[b]
                g[a] = jnp.where(low, ga, pltpu.roll(gb, 32, 1))
                g[b] = jnp.where(low, pltpu.roll(ga, 96, 1), gb)
            turned4.append(g)
        for sub in range(4):
            k = 4 * t + sub
            last = turned4[3][sub].reshape(2, 8, 128)
            for s in range(3):
                tile = turned4[s][sub].reshape(2, 8, 128)
                tile = jnp.where(row8 >= 6, pltpu.roll(last, 6 - 2 * s, 1), tile)
                msg[k, :, 128 * s : 128 * s + 128] = tile.reshape(16, 128).astype(BF16)
        return carry

    lax.fori_loop(0, TILES, pack, 0)
    land[chip] = msg[chip]

    def edge_pack(n, start):
        whole = jnp.zeros((16, 128), F32)
        for az in range(AZ):
            v = [ext[line, az, :, start : start + 128].astype(F32) for line in range(2)]
            re = jnp.concatenate([v[0][0:8], v[1][0:8]], axis=0)
            im = jnp.concatenate([v[0][8:16], v[1][8:16]], axis=0)
            for s in range(3 if az == 4 else 1):
                to = 32 * s if az == 4 else 32 * ((az + 2) % 4)
                here = jnp.where(in32 < 16, pltpu.roll(re, 10 + to, 1), pltpu.roll(im, (26 + to) % 128, 1))
                if az == 4:
                    here = pltpu.roll(here.reshape(2, 8, 128), 6 - 2 * s, 1).reshape(16, 128)
                    keep = (lanes // 32 == s) & (row8.reshape(16, 128) >= 6)
                else:
                    keep = lanes // 32 == to // 32
                whole = jnp.where(keep, here, whole)
        edge_msg[n] = whole.astype(BF16)

    def edge_copy(n, to, row):
        return pltpu.make_async_remote_copy(
            src_ref=edge_msg.at[n], dst_ref=edge.at[chip], send_sem=edge_send.at[n], recv_sem=edge_recv,
            device_id={"scene": 2 * to + c, "strip": row}, device_id_type=MESH,
        )

    edge_pack(0, 1024)
    edge_pack(1, 128)
    sides = jnp.where(y < STRIPS - 1, 1, 0) + jnp.where(y > 0, 1, 0)
    pl.semaphore_wait(barrier, CHIPS + sides)

    @pl.when(y < STRIPS - 1)
    def _():
        edge_copy(0, 0, y + 1).start()

    @pl.when(y > 0)
    def _():
        edge_copy(1, CHIPS - 1, y - 1).start()

    order = [across(x, i // ZS) * ZS + along(z, i % ZS) for i in range(CHIPS - 1)]

    def data_copy(i, src, dst, to):
        return pltpu.make_async_remote_copy(
            src_ref=src, dst_ref=dst, send_sem=data_send, recv_sem=data_recv.at[i],
            device_id={"scene": 2 * to + c}, device_id_type=MESH,
        )

    def list_copy(src, dst, to):
        return pltpu.make_async_remote_copy(
            src_ref=src, dst_ref=dst, send_sem=list_send, recv_sem=list_recv,
            device_id={"scene": 2 * to + c}, device_id_type=MESH,
        )

    for i in range(ZS):
        data_copy(i // ZS, msg.at[order[i]], land.at[chip], order[i]).start()
    for i in range(CHIPS - 1):
        list_copy(own_list, lists.at[chip], order[i]).start()
    for i in range(ZS, CHIPS - 1):
        data_copy(i // ZS, msg.at[order[i]], land.at[chip], order[i]).start()

    gets[4].wait()
    gets[5].wait()

    rows = lax.broadcasted_iota(jnp.int32, (512, 320), 0)
    place = lax.rem(rows, 8)
    slot = (rows // 16) * 12 + (lax.rem(rows, 16) // 8) * 6 + place
    slot = jnp.where(place < SLOTS, slot, -7)
    lane = lax.broadcasted_iota(jnp.int32, (512, 320), 1).astype(F32)
    scene = jnp.sum(jnp.where(slot == slot_ref[...].reshape(1, 320), lane + 1.0, 0.0), axis=1, keepdims=True) - 1.0
    scene_k[...] = jnp.broadcast_to(scene, (512, 128)).astype(jnp.int32)

    lists[chip] = own_list[...]

    def hand(i):
        first = across(x, i) * ZS
        many = ZS if i < XS - 1 else ZS - 1
        data_copy(i, msg.at[pl.ds(0, many)], land.at[pl.ds(first, many)], chip).wait_recv()
        copy = pltpu.make_async_remote_copy(
            src_ref=land.at[pl.ds(first, ZS)], dst_ref=par.at[pl.ds(first, ZS)],
            send_sem=hand_send.at[i], recv_sem=hand_recv.at[i], device_id=partner, device_id_type=MESH,
        )
        copy.start()
        return copy

    most = pl.ds(0, CHIPS - 1)
    list_copy(lists.at[most], lists.at[most], chip).wait_recv()
    hand_list = pltpu.make_async_remote_copy(
        src_ref=lists, dst_ref=lists_par, send_sem=core_send.at[0], recv_sem=core_recv.at[0],
        device_id=partner, device_id_type=MESH,
    )
    hand_list.start()
    hands = [hand(0)]
    hand_list.wait_recv()

    half = lax.broadcasted_iota(jnp.int32, (2, 128), 1) // 64

    def one_hot(m, carry):
        for n in range(2):
            pair = jnp.where(half == c, lists[2 * m + n], lists_par[2 * m + n])
            for part in range(2):
                hit = jnp.where(scene_k[...] == pair[part : part + 1, :], 1.0, 0.0).astype(BF16)
                hot[m, :, 256 * part + 128 * n : 256 * part + 128 * n + 128] = hit
        return carry

    lax.fori_loop(0, CHIPS // 2, one_hot, 0)
    hands.append(hand(1))
    hand_edge = pltpu.make_async_remote_copy(
        src_ref=edge, dst_ref=edge_par, send_sem=core_send.at[1], recv_sem=core_recv.at[1],
        device_id=partner, device_id_type=MESH,
    )

    @pl.when(at_left | at_right)
    def _():
        pltpu.make_async_remote_copy(
            src_ref=edge, dst_ref=edge, send_sem=edge_send.at[0], recv_sem=edge_recv,
            device_id={"scene": 2 * chip + c, "strip": side}, device_id_type=MESH,
        ).wait_recv()
        hand_edge.start()

    hands.append(hand(2))
    hands.append(hand(3))
    for copy in hands:
        copy.wait_recv()

    def line_of(mine, others):
        a, b = (v.astype(F32).reshape(CHIPS, 2, 8, 128) for v in (mine, others))
        a = jnp.where(c == 0, a[:, 0], a[:, 1])
        b = jnp.where(c == 0, b[:, 0], b[:, 1])
        pair = [jnp.where(c == 0, a, b), jnp.where(c == 0, b, a)]
        return jnp.stack(pair, axis=1).reshape(64, 8, 128)

    wide = [line_of(*(r[:, :, 128 * s : 128 * s + 128] for r in (land, par))) for s in range(3)]
    part = [v.reshape(512, 128).astype(BF16) for v in wide]
    row = lax.broadcasted_iota(jnp.int32, (64, 8, 128), 1)
    last = jnp.where(
        row < 2, pltpu.roll(wide[0], 2, 1), jnp.where(row < 4, pltpu.roll(wide[1], 4, 1), pltpu.roll(wide[2], 6, 1))
    )
    sent[...] = jnp.concatenate(part + [last.reshape(512, 128).astype(BF16)], axis=1)

    @pl.when(at_left | at_right)
    def _():
        hand_edge.wait()
        lane = lax.broadcasted_iota(jnp.int32, (512, 128), 1)
        left = jnp.where(chip == 0, 1, 0)
        ours = jnp.where(lax.rem(lane, 16) < 10, left, 1 - left) == 1
        fold = line_of(edge[...], edge_par[...])
        got = fold.reshape(512, 128)
        deep = [pltpu.roll(fold, 2 * s + 2, 1).reshape(512, 128) for s in range(3)]
        deep = [pltpu.roll(deep[s], 64 - 32 * s, 1) for s in range(3)]
        level = row.reshape(512, 128)
        deep = jnp.where(level < 2, deep[0], jnp.where(level < 4, deep[1], deep[2]))
        third, fourth = sent[:, 256:384].astype(F32), sent[:, 384:512].astype(F32)
        sent[:, 256:384] = jnp.where(ours & (lane >= 64), got, third).astype(BF16)
        sent[:, 384:512] = jnp.where(ours, jnp.where(lane < 64, got, deep), fourth).astype(BF16)

    feat[...] = lax.dot_general(
        order_ref[...], sent[...], (((1,), (1,)), ((), ())), preferred_element_type=F32
    ).astype(BF16)

    def back_copy(i, src, dst, to):
        return pltpu.make_async_remote_copy(
            src_ref=src, dst_ref=dst, send_sem=back_send, recv_sem=back_recv.at[i],
            device_id={"scene": 2 * to + c}, device_id_type=MESH,
        )

    def step_of(i):
        zp = lax.rem(z // 2 + far_first(lax.rem(i, 4)), 4)
        return across(x, i // 4) * 4 + zp

    def gather(ref, i):
        ref[...] = jnp.dot(feat[...], hot[step_of(i)], preferred_element_type=F32)

    def sums(ref, i):
        for n in range(2):
            p, q = slice(128 * n, 128 * n + 128), slice(256 + 128 * n, 384 + 128 * n)
            main, halo = [0.0] * 4, [0.0] * 4
            for az in range(AZ):
                a0, b0 = ref[96 * az : 96 * az + 48, p], ref[96 * az : 96 * az + 48, q]
                a1, b1 = ref[96 * az + 48 : 96 * az + 96, p], ref[96 * az + 48 : 96 * az + 96, q]
                planes = (a0 * b0 + a1 * b1, a1 * b0 - a0 * b1, a0 * a0 + a1 * a1, b0 * b0 + b1 * b1)
                for m, plane in enumerate(planes):
                    for w in range(4):
                        main[m] = main[m] + plane[8 * w : 8 * w + 8]
                    for w in range(4, 6):
                        halo[m] = halo[m] + plane[8 * w : 8 * w + 8]
            looks = [windows(u, v + pltpu.roll(v, 4, 0)) for u, v in zip(main, halo)]
            scale = lax.rsqrt(looks[2] * looks[3] + 1e-06)
            value = jnp.concatenate([looks[0] * scale, looks[1] * scale], axis=0)
            res[2 * step_of(i) + n] = value


    def compute(j, carry):
        i = 2 * j
        gather(both_a, i)
        sums(both_a, i)
        gather(both_b, i + 1)
        sums(both_b, i + 1)
        for n in range(4):
            k = 2 * step_of(i + n // 2) + n % 2

            @pl.when(k != chip)
            def _():
                back_copy(j // 2, res.at[k], back.at[chip], k).start()
        return carry

    lax.fori_loop(0, CHIPS // 4, compute, 0)
    back[chip] = res[chip]

    gives = []
    for n in range(2):
        h = (x // 2 + 1 + n) % 2
        for i in (2 * n, 2 * n + 1):
            some = pl.ds(0, ZS if i < XS - 1 else ZS - 1)
            back_copy(i, res.at[some], back.at[some], chip).wait_recv()
        for ri in range(2):
            turned[h, ri] = back[pl.ds(16 * h, 16), 8 * ri : 8 * ri + 8, :].reshape(128, 128).T
        give = pltpu.make_async_remote_copy(
            src_ref=turned.at[h, :, pl.ds(pl.multiple_of(64 * other, 64), 64), :], dst_ref=fin.at[h],
            send_sem=fin_send.at[n], recv_sem=fin_recv.at[n], device_id=partner, device_id_type=MESH,
        )
        give.start()
        gives.append(give)
    for h in range(2):
        out_ref[c, :, :, 128 * h : 128 * h + 128] = turned[h, :, pl.ds(pl.multiple_of(64 * c, 64), 64), :]
    for copy in hands + [hand_list]:
        copy.wait_send()
    for give in gives:
        give.wait()
    for h in range(2):
        out_ref[other, :, :, 128 * h : 128 * h + 128] = fin[h]

    @pl.when(y < STRIPS - 1)
    def _():
        edge_copy(0, 0, y + 1).wait_send()

    @pl.when(y > 0)
    def _():
        edge_copy(1, CHIPS - 1, y - 1).wait_send()

    list_copy(lists.at[most], lists.at[most], chip).wait_send()
    data_copy(0, msg.at[most], land.at[most], chip).wait_send()
    back_copy(0, res.at[most], back.at[most], chip).wait_send()


def shards(scene_tiles, scene_slot, pair_ref, pair_sec, pair_count):
    pcap = pair_ref.shape[0]
    order = jnp.asarray(feature_order(), BF16)
    vmem = pl.BlockSpec(memory_space=pltpu.VMEM)
    dma = pltpu.SemaphoreType.DMA
    arrays = (
        scene_tiles, scene_slot, pair_ref.reshape(1, pcap), pair_sec.reshape(1, pcap),
        pair_count.reshape(1, 1), order,
    )
    out = pl.pallas_call(
        kernel,
        out_shape=jax.ShapeDtypeStruct((2, 2, pcap, 256), F32),
        in_specs=[pl.BlockSpec(memory_space=pltpu.HBM)] * 6,
        out_specs=vmem,
        scratch_shapes=[
            pltpu.VMEM((320,), jnp.int32),
            pltpu.VMEM((1, 64), jnp.int32),
            pltpu.VMEM((1, 64), jnp.int32),
            pltpu.VMEM((1, 1), jnp.int32),
            pltpu.VMEM((ROWS, 512), BF16),
            pltpu.VMEM(scene_tiles.shape, BF16),
            pltpu.VMEM((2, AZ, 16, 1280), BF16),
            pltpu.VMEM((CHIPS, 16, 128), BF16),
            pltpu.VMEM((CHIPS, 16, 128), BF16),
            pltpu.VMEM((2, 16, 128), BF16),
            pltpu.VMEM((512, 512), BF16),
            pltpu.VMEM((CHIPS, 16, 384), BF16),
            pltpu.VMEM((CHIPS, 16, 384), BF16),
            pltpu.VMEM((CHIPS, 16, 384), BF16),
            pltpu.VMEM((2, 128), jnp.int32),
            pltpu.VMEM((CHIPS, 2, 128), jnp.int32),
            pltpu.VMEM((CHIPS, 2, 128), jnp.int32),
            pltpu.VMEM((512, 128), jnp.int32),
            pltpu.VMEM((CHIPS // 2, 512, 512), BF16),
            pltpu.VMEM((ROWS, 512), BF16),
            pltpu.VMEM((ROWS, 512), F32),
            pltpu.VMEM((ROWS, 512), F32),
            pltpu.VMEM((CHIPS, 16, 128), F32),
            pltpu.VMEM((CHIPS, 16, 128), F32),
            pltpu.VMEM((2, 2, 128, 128), F32),
            pltpu.VMEM((2, 2, 64, 128), F32),
            dma((6,)), dma((2,)), dma((2,)), dma((XS,)), dma((XS,)), dma((2,)), dma, dma, dma,
            dma, dma((XS,)), dma, dma((XS,)), dma((2,)), dma((2,)),
        ],
        compiler_params=pltpu.CompilerParams(
            collective_id=0, has_side_effects=True, vmem_limit_bytes=40 << 20
        ),
        name="coherence",
    )(*(v if v.size == 1 else pltpu.with_memory_space_constraint(v, pltpu.HBM) for v in arrays))
    return out.transpose(2, 0, 1, 3)


def solution(mesh):
    placed = (P("scene", None, None, "strip"), P(), P("scene"), P("scene"), P("scene"))
    return jax.shard_map(
        shards,
        mesh=mesh,
        in_specs=placed,
        out_specs=P("scene", None, None, "strip"),
        check_vma=False,
    )
```

```python
import functools

import jax
import jax.numpy as jnp
import numpy as np
from jax import lax
from jax.experimental import pallas as pl
from jax.experimental.pallas import tpu as pltpu
from jax.sharding import PartitionSpec as P

MESH = pl.DeviceIdType.MESH
F32 = jnp.float32
BF16 = jnp.bfloat16

XS, ZS, CHIPS = 4, 8, 32
STRIPS = 4
SLOTS = 6
AZ = 5
TILES = 8
ROWS = 480


def feature_order():
    order = np.zeros((ROWS, 512), np.float32)
    for az in range(AZ):
        for ri in range(2):
            for cell in range(-10, 38):
                block, w = (cell + 2) // 4, (cell + 2) % 4
                base = 96 * az + 48 * ri
                if 0 <= block < 8:
                    row = base + 8 * w + block
                else:
                    row = base + 32 + 4 * w + {-2: 0, -1: 1, 8: 2, 9: 3}[block]
                if 0 <= cell < 32:
                    lane = 32 * (2 * az + ri) + cell
                else:
                    h = cell + 10 if cell < 0 else cell - 22
                    lane = 32 * (10 + az) + 16 * ri + h
                order[row, lane] = 1.0
    return order


def far_first(i):
    return jnp.where(i == 0, 2, jnp.where(i == 1, 1, jnp.where(i == 2, 3, 0)))


def across(x, i):
    low = lax.rem(x, 2)
    high = x // 2
    flip = jnp.where(lax.rem(i, 3) == 0, low, 1 - low)
    return jnp.where(i < 2, 1 - high, high) * 2 + flip


def along(z, j):
    step = (j + 1) // 2
    return lax.rem(z + jnp.where(lax.rem(j, 2) == 0, ZS // 2 + step, ZS // 2 - step), ZS)


def both_parts(v):
    rows = jnp.zeros((2, v.shape[-1]), F32)
    v = v.astype(F32)
    return jnp.concatenate([v[:, 0, :], rows, v[:, 1, :], rows], axis=0).astype(BF16)


def windows(main, halo):
    row = lax.broadcasted_iota(jnp.int32, main.shape, 0)
    total = main + jnp.where(row < 1, pltpu.roll(halo, 7, 0), pltpu.roll(main, 1, 0))
    total += jnp.where(row < 2, halo, pltpu.roll(main, 2, 0))
    total += jnp.where(row >= 7, pltpu.roll(halo, 1, 0), pltpu.roll(main, 7, 0))
    total += jnp.where(row >= 6, halo, pltpu.roll(main, 6, 0))
    return total


def kernel(
    tiles_hbm, slot_hbm, ref_hbm, sec_hbm, count_hbm, order_hbm, out_ref,
    slot_ref, ref_ref, sec_ref, count_ref, order_ref, raw, ext, edge, edge_par, edge_msg, sent, msg, land, par,
    own_list, lists, lists_par, scene_k, hot, feat, both_a, both_b,
    res, back, turned, fin,
    in_sem, core_send, core_recv, hand_send, hand_recv, edge_send, edge_recv, list_send, list_recv,
    data_send, data_recv, back_send, back_recv, fin_send, fin_recv,
):
    me = lax.axis_index("scene")
    y = lax.axis_index("strip")
    chip, c = me // 2, lax.rem(me, 2)
    other = 1 - c
    x, z = chip // ZS, lax.rem(chip, ZS)
    partner = {"scene": chip * 2 + other}

    barrier = pltpu.get_barrier_semaphore()

    order = [across(x, i // ZS) * ZS + along(z, i % ZS) for i in range(CHIPS - 1)]
    for k in order:
        pl.semaphore_signal(barrier, inc=1, device_id={"scene": 2 * k + c}, device_id_type=MESH)
    pl.semaphore_signal(barrier, inc=1, device_id=partner, device_id_type=MESH)

    at_left = (chip == 0) & (y > 0)
    at_right = (chip == CHIPS - 1) & (y < STRIPS - 1)
    side = jnp.where(chip == 0, y - 1, y + 1)

    def greet_side(k, carry):
        pl.semaphore_signal(
            barrier, inc=1, device_id={"scene": 2 * k + c, "strip": side}, device_id_type=MESH
        )
        return carry

    @pl.when(at_left | at_right)
    def _():
        lax.fori_loop(0, CHIPS, greet_side, 0)

    gets = [
        pltpu.make_async_copy(src, dst, in_sem.at[n])
        for n, (src, dst) in enumerate((
            (tiles_hbm, raw), (ref_hbm, ref_ref), (sec_hbm, sec_ref), (count_hbm, count_ref),
            (slot_hbm, slot_ref), (order_hbm, order_ref),
        ))
    ]
    for get in gets:
        get.start()
    for get in gets[1:4]:
        get.wait()
    mine = lax.broadcasted_iota(jnp.int32, (1, 64), 1) < count_ref[...]
    for n, ref in enumerate((ref_ref, sec_ref)):
        pair = jnp.where(mine, ref[...], -2)
        own_list[n : n + 1, 0:64] = pair
        own_list[n : n + 1, 64:128] = pair
    ext[:, :, :, 0:128] = jnp.zeros((2, AZ, 16, 128), BF16)
    ext[:, :, :, 1152:1280] = jnp.zeros((2, AZ, 16, 128), BF16)
    gets[0].wait()

    def lines(az, carry):
        for line in range(2):
            ext[line, az, :, 128:1152] = both_parts(raw[:, AZ * line + az])
        return carry

    lax.fori_loop(0, AZ, lines, 0)

    lanes = lax.broadcasted_iota(jnp.int32, (16, 128), 1)
    in32 = lax.rem(lanes, 32)
    row8 = lax.broadcasted_iota(jnp.int32, (2, 8, 128), 1)

    def pack(t, carry):
        at = pl.ds(pl.multiple_of(t * 128, 128), 384)
        groups, halos = [], []
        for az in range(AZ):
            v = [ext[line, az, :, at].astype(F32) for line in range(2)]
            re = jnp.concatenate([v[0][0:8], v[1][0:8]], axis=0)
            im = jnp.concatenate([v[0][8:16], v[1][8:16]], axis=0)
            groups += [re[:, 128:256], im[:, 128:256]]
            near = jnp.where(in32 < 10, pltpu.roll(re, 10, 1)[:, 128:256], pltpu.roll(re, 384 - 22, 1)[:, 128:256])
            far = jnp.where(in32 < 26, pltpu.roll(im, 26, 1)[:, 128:256], pltpu.roll(im, 384 - 6, 1)[:, 128:256])
            halos.append(jnp.where(in32 < 16, near, far))
        groups += halos + [jnp.zeros((16, 128), F32)]
        turned4 = []
        for s in range(4):
            g = groups[4 * s : 4 * s + 4]
            low = lanes < 64
            for a, b in ((0, 2), (1, 3)):
                ga, gb = g[a], g[b]
                g[a] = jnp.where(low, ga, pltpu.roll(gb, 64, 1))
                g[b] = jnp.where(low, pltpu.roll(ga, 64, 1), gb)
            low = lax.rem(lanes, 64) < 32
            for a, b in ((0, 1), (2, 3)):
                ga, gb = g[a], g[b]
                g[a] = jnp.where(low, ga, pltpu.roll(gb, 32, 1))
                g[b] = jnp.where(low, pltpu.roll(ga, 96, 1), gb)
            turned4.append(g)
        for sub in range(4):
            k = 4 * t + sub
            last = turned4[3][sub].reshape(2, 8, 128)
            for s in range(3):
                tile = turned4[s][sub].reshape(2, 8, 128)
                tile = jnp.where(row8 >= 6, pltpu.roll(last, 6 - 2 * s, 1), tile)
                msg[k, :, 128 * s : 128 * s + 128] = tile.reshape(16, 128).astype(BF16)
        return carry

    lax.fori_loop(0, TILES, pack, 0)
    land[chip] = msg[chip]

    def edge_pack(n, start):
        whole = jnp.zeros((16, 128), F32)
        for az in range(AZ):
            v = [ext[line, az, :, start : start + 128].astype(F32) for line in range(2)]
            re = jnp.concatenate([v[0][0:8], v[1][0:8]], axis=0)
            im = jnp.concatenate([v[0][8:16], v[1][8:16]], axis=0)
            for s in range(3 if az == 4 else 1):
                to = 32 * s if az == 4 else 32 * ((az + 2) % 4)
                here = jnp.where(in32 < 16, pltpu.roll(re, 10 + to, 1), pltpu.roll(im, (26 + to) % 128, 1))
                if az == 4:
                    here = pltpu.roll(here.reshape(2, 8, 128), 6 - 2 * s, 1).reshape(16, 128)
                    keep = (lanes // 32 == s) & (row8.reshape(16, 128) >= 6)
                else:
                    keep = lanes // 32 == to // 32
                whole = jnp.where(keep, here, whole)
        edge_msg[n] = whole.astype(BF16)

    def edge_copy(n, to, row):
        return pltpu.make_async_remote_copy(
            src_ref=edge_msg.at[n], dst_ref=edge.at[chip], send_sem=edge_send.at[n], recv_sem=edge_recv,
            device_id={"scene": 2 * to + c, "strip": row}, device_id_type=MESH,
        )

    edge_pack(0, 1024)
    edge_pack(1, 128)
    sides = jnp.where(y < STRIPS - 1, 1, 0) + jnp.where(y > 0, 1, 0)
    pl.semaphore_wait(barrier, CHIPS + sides)

    @pl.when(y < STRIPS - 1)
    def _():
        edge_copy(0, 0, y + 1).start()

    @pl.when(y > 0)
    def _():
        edge_copy(1, CHIPS - 1, y - 1).start()

    def data_copy(i, src, dst, to):
        return pltpu.make_async_remote_copy(
            src_ref=src, dst_ref=dst, send_sem=data_send, recv_sem=data_recv.at[i],
            device_id={"scene": 2 * to + c}, device_id_type=MESH,
        )

    def list_copy(src, dst, to):
        return pltpu.make_async_remote_copy(
            src_ref=src, dst_ref=dst, send_sem=list_send, recv_sem=list_recv,
            device_id={"scene": 2 * to + c}, device_id_type=MESH,
        )

    for i in range(ZS):
        data_copy(i // ZS, msg.at[order[i]], land.at[chip], order[i]).start()
    for i in range(CHIPS - 1):
        list_copy(own_list, lists.at[chip], order[i]).start()
    for i in range(ZS, CHIPS - 1):
        data_copy(i // ZS, msg.at[order[i]], land.at[chip], order[i]).start()

    gets[4].wait()
    gets[5].wait()

    rows = lax.broadcasted_iota(jnp.int32, (512, 320), 0)
    place = lax.rem(rows, 8)
    slot = (rows // 16) * 12 + (lax.rem(rows, 16) // 8) * 6 + place
    slot = jnp.where(place < SLOTS, slot, -7)
    lane = lax.broadcasted_iota(jnp.int32, (512, 320), 1).astype(F32)
    scene = jnp.sum(jnp.where(slot == slot_ref[...].reshape(1, 320), lane + 1.0, 0.0), axis=1, keepdims=True) - 1.0
    scene_k[...] = jnp.broadcast_to(scene, (512, 128)).astype(jnp.int32)

    lists[chip] = own_list[...]

    def hand(i):
        first = across(x, i) * ZS
        many = ZS if i < XS - 1 else ZS - 1
        data_copy(i, msg.at[pl.ds(0, many)], land.at[pl.ds(first, many)], chip).wait_recv()
        copy = pltpu.make_async_remote_copy(
            src_ref=land.at[pl.ds(first, ZS)], dst_ref=par.at[pl.ds(first, ZS)],
            send_sem=hand_send.at[i], recv_sem=hand_recv.at[i], device_id=partner, device_id_type=MESH,
        )
        copy.start()
        return copy

    most = pl.ds(0, CHIPS - 1)
    list_copy(lists.at[most], lists.at[most], chip).wait_recv()
    hand_list = pltpu.make_async_remote_copy(
        src_ref=lists, dst_ref=lists_par, send_sem=core_send.at[0], recv_sem=core_recv.at[0],
        device_id=partner, device_id_type=MESH,
    )
    hand_list.start()
    hands = [hand(0)]
    hand_list.wait_recv()

    half = lax.broadcasted_iota(jnp.int32, (2, 128), 1) // 64

    def one_hot(m, carry):
        for n in range(2):
            pair = jnp.where(half == c, lists[2 * m + n], lists_par[2 * m + n])
            for part in range(2):
                hit = jnp.where(scene_k[...] == pair[part : part + 1, :], 1.0, 0.0).astype(BF16)
                hot[m, :, 256 * part + 128 * n : 256 * part + 128 * n + 128] = hit
        return carry

    lax.fori_loop(0, CHIPS // 2, one_hot, 0)
    hands.append(hand(1))
    hand_edge = pltpu.make_async_remote_copy(
        src_ref=edge, dst_ref=edge_par, send_sem=core_send.at[1], recv_sem=core_recv.at[1],
        device_id=partner, device_id_type=MESH,
    )

    @pl.when(at_left | at_right)
    def _():
        pltpu.make_async_remote_copy(
            src_ref=edge, dst_ref=edge, send_sem=edge_send.at[0], recv_sem=edge_recv,
            device_id={"scene": 2 * chip + c, "strip": side}, device_id_type=MESH,
        ).wait_recv()
        hand_edge.start()

    hands.append(hand(2))
    hands.append(hand(3))
    for copy in hands:
        copy.wait_recv()

    def line_of(mine, others):
        a, b = (v.astype(F32).reshape(CHIPS, 2, 8, 128) for v in (mine, others))
        a = jnp.where(c == 0, a[:, 0], a[:, 1])
        b = jnp.where(c == 0, b[:, 0], b[:, 1])
        pair = [jnp.where(c == 0, a, b), jnp.where(c == 0, b, a)]
        return jnp.stack(pair, axis=1).reshape(64, 8, 128)

    wide = [line_of(*(r[:, :, 128 * s : 128 * s + 128] for r in (land, par))) for s in range(3)]
    part = [v.reshape(512, 128).astype(BF16) for v in wide]
    row = lax.broadcasted_iota(jnp.int32, (64, 8, 128), 1)
    last = jnp.where(
        row < 2, pltpu.roll(wide[0], 2, 1), jnp.where(row < 4, pltpu.roll(wide[1], 4, 1), pltpu.roll(wide[2], 6, 1))
    )
    sent[...] = jnp.concatenate(part + [last.reshape(512, 128).astype(BF16)], axis=1)

    @pl.when(at_left | at_right)
    def _():
        hand_edge.wait()
        lane = lax.broadcasted_iota(jnp.int32, (512, 128), 1)
        left = jnp.where(chip == 0, 1, 0)
        ours = jnp.where(lax.rem(lane, 16) < 10, left, 1 - left) == 1
        fold = line_of(edge[...], edge_par[...])
        got = fold.reshape(512, 128)
        deep = [pltpu.roll(fold, 2 * s + 2, 1).reshape(512, 128) for s in range(3)]
        deep = [pltpu.roll(deep[s], 64 - 32 * s, 1) for s in range(3)]
        level = row.reshape(512, 128)
        deep = jnp.where(level < 2, deep[0], jnp.where(level < 4, deep[1], deep[2]))
        third, fourth = sent[:, 256:384].astype(F32), sent[:, 384:512].astype(F32)
        sent[:, 256:384] = jnp.where(ours & (lane >= 64), got, third).astype(BF16)
        sent[:, 384:512] = jnp.where(ours, jnp.where(lane < 64, got, deep), fourth).astype(BF16)

    feat[...] = lax.dot_general(
        order_ref[...], sent[...], (((1,), (1,)), ((), ())), preferred_element_type=F32
    ).astype(BF16)

    def back_copy(i, src, dst, to):
        return pltpu.make_async_remote_copy(
            src_ref=src, dst_ref=dst, send_sem=back_send, recv_sem=back_recv.at[i],
            device_id={"scene": 2 * to + c}, device_id_type=MESH,
        )

    def step_of(i):
        zp = lax.rem(z // 2 + far_first(lax.rem(i, 4)), 4)
        return across(x, i // 4) * 4 + zp

    def gather(ref, i):
        ref[...] = jnp.dot(feat[...], hot[step_of(i)], preferred_element_type=F32)

    def sums(ref, i):
        for n in range(2):
            p, q = slice(128 * n, 128 * n + 128), slice(256 + 128 * n, 384 + 128 * n)
            main, halo = [0.0] * 4, [0.0] * 4
            for az in range(AZ):
                a0, b0 = ref[96 * az : 96 * az + 48, p], ref[96 * az : 96 * az + 48, q]
                a1, b1 = ref[96 * az + 48 : 96 * az + 96, p], ref[96 * az + 48 : 96 * az + 96, q]
                planes = (a0 * b0 + a1 * b1, a1 * b0 - a0 * b1, a0 * a0 + a1 * a1, b0 * b0 + b1 * b1)
                for m, plane in enumerate(planes):
                    for w in range(4):
                        main[m] = main[m] + plane[8 * w : 8 * w + 8]
                    for w in range(4, 6):
                        halo[m] = halo[m] + plane[8 * w : 8 * w + 8]
            looks = [windows(u, v + pltpu.roll(v, 4, 0)) for u, v in zip(main, halo)]
            scale = lax.rsqrt(looks[2] * looks[3] + 1e-06)
            value = jnp.concatenate([looks[0] * scale, looks[1] * scale], axis=0)
            res[2 * step_of(i) + n] = value


    def compute(j, carry):
        i = 2 * j
        gather(both_a, i)
        sums(both_a, i)
        gather(both_b, i + 1)
        sums(both_b, i + 1)
        for n in range(4):
            k = 2 * step_of(i + n // 2) + n % 2

            @pl.when(k != chip)
            def _():
                back_copy(j // 2, res.at[k], back.at[chip], k).start()
        return carry

    lax.fori_loop(0, CHIPS // 4, compute, 0)
    back[chip] = res[chip]

    gives = []
    for n in range(2):
        h = (x // 2 + 1 + n) % 2
        for i in (2 * n, 2 * n + 1):
            some = pl.ds(0, ZS if i < XS - 1 else ZS - 1)
            back_copy(i, res.at[some], back.at[some], chip).wait_recv()
        for ri in range(2):
            turned[h, ri] = back[pl.ds(16 * h, 16), 8 * ri : 8 * ri + 8, :].reshape(128, 128).T
        give = pltpu.make_async_remote_copy(
            src_ref=turned.at[h, :, pl.ds(pl.multiple_of(64 * other, 64), 64), :], dst_ref=fin.at[h],
            send_sem=fin_send.at[n], recv_sem=fin_recv.at[n], device_id=partner, device_id_type=MESH,
        )
        give.start()
        gives.append(give)
    for h in range(2):
        out_ref[c, :, :, 128 * h : 128 * h + 128] = turned[h, :, pl.ds(pl.multiple_of(64 * c, 64), 64), :]
    for copy in hands + [hand_list]:
        copy.wait_send()
    for give in gives:
        give.wait()
    for h in range(2):
        out_ref[other, :, :, 128 * h : 128 * h + 128] = fin[h]

    @pl.when(y < STRIPS - 1)
    def _():
        edge_copy(0, 0, y + 1).wait_send()

    @pl.when(y > 0)
    def _():
        edge_copy(1, CHIPS - 1, y - 1).wait_send()

    list_copy(lists.at[most], lists.at[most], chip).wait_send()
    data_copy(0, msg.at[most], land.at[most], chip).wait_send()
    back_copy(0, res.at[most], back.at[most], chip).wait_send()


def shards(scene_tiles, scene_slot, pair_ref, pair_sec, pair_count):
    pcap = pair_ref.shape[0]
    order = jnp.asarray(feature_order(), BF16)
    vmem = pl.BlockSpec(memory_space=pltpu.VMEM)
    dma = pltpu.SemaphoreType.DMA
    arrays = (
        scene_tiles, scene_slot, pair_ref.reshape(1, pcap), pair_sec.reshape(1, pcap),
        pair_count.reshape(1, 1), order,
    )
    out = pl.pallas_call(
        kernel,
        out_shape=jax.ShapeDtypeStruct((2, 2, pcap, 256), F32),
        in_specs=[pl.BlockSpec(memory_space=pltpu.HBM)] * 6,
        out_specs=vmem,
        scratch_shapes=[
            pltpu.VMEM((320,), jnp.int32),
            pltpu.VMEM((1, 64), jnp.int32),
            pltpu.VMEM((1, 64), jnp.int32),
            pltpu.VMEM((1, 1), jnp.int32),
            pltpu.VMEM((ROWS, 512), BF16),
            pltpu.VMEM(scene_tiles.shape, BF16),
            pltpu.VMEM((2, AZ, 16, 1280), BF16),
            pltpu.VMEM((CHIPS, 16, 128), BF16),
            pltpu.VMEM((CHIPS, 16, 128), BF16),
            pltpu.VMEM((2, 16, 128), BF16),
            pltpu.VMEM((512, 512), BF16),
            pltpu.VMEM((CHIPS, 16, 384), BF16),
            pltpu.VMEM((CHIPS, 16, 384), BF16),
            pltpu.VMEM((CHIPS, 16, 384), BF16),
            pltpu.VMEM((2, 128), jnp.int32),
            pltpu.VMEM((CHIPS, 2, 128), jnp.int32),
            pltpu.VMEM((CHIPS, 2, 128), jnp.int32),
            pltpu.VMEM((512, 128), jnp.int32),
            pltpu.VMEM((CHIPS // 2, 512, 512), BF16),
            pltpu.VMEM((ROWS, 512), BF16),
            pltpu.VMEM((ROWS, 512), F32),
            pltpu.VMEM((ROWS, 512), F32),
            pltpu.VMEM((CHIPS, 16, 128), F32),
            pltpu.VMEM((CHIPS, 16, 128), F32),
            pltpu.VMEM((2, 2, 128, 128), F32),
            pltpu.VMEM((2, 2, 64, 128), F32),
            dma((6,)), dma((2,)), dma((2,)), dma((XS,)), dma((XS,)), dma((2,)), dma, dma, dma,
            dma, dma((XS,)), dma, dma((XS,)), dma((2,)), dma((2,)),
        ],
        compiler_params=pltpu.CompilerParams(
            collective_id=0, has_side_effects=True, vmem_limit_bytes=40 << 20
        ),
        name="coherence",
    )(*(v if v.size == 1 else pltpu.with_memory_space_constraint(v, pltpu.HBM) for v in arrays))
    return out.transpose(2, 0, 1, 3)


def solution(mesh):
    placed = (P("scene", None, None, "strip"), P(), P("scene"), P("scene"), P("scene"))
    return jax.shard_map(
        shards,
        mesh=mesh,
        in_specs=placed,
        out_specs=P("scene", None, None, "strip"),
        check_vma=False,
    )
```
